32 devices in a mesh: dev: 32 (over z, y, x, core).
Axes of the slice: x: 2, y: 2, z: 4, core: 2. Of those that a mesh axis runs over, the one named last changes fastest.
Arguments:
- embeddings: bfloat16 [8192, 1024], P('dev'), may hold values from -6 to 6
- cluster_id: int32 [8192], P('dev'), may hold values from 0 to 15, as said below
- requests: int32 [1024], P('dev'), may hold values from -1 to 1, as said below
- pair_left: int32 [12288], P('dev'), may hold values from 0 to 31, as said below
- pair_right: int32 [12288], P('dev'), may hold values from 0 to 31, as said below
Outputs:
- best: float32 [8192], P('dev')
The draws below stay inside these ranges and needn't reach their ends.
Inputs may be any that keep to these rules, and one draw needn't show every extreme that they name: Rows are sorted by cluster: cluster_id never falls along the rows, and every cluster has rows. Every slot that some task of device d names has a block (requests at least 0 there); a device's tasks name slots of at most 32 consecutive owners. pair_left <= pair_right for every task; no device lists one slot pair twice. `pair_right`: see pair_left.
All inputs are finite; a program needn't handle non-finite values.
Results may differ from the reference program's by a relative error of at most 0.00086.
Values may be sent and summed in bfloat16 or wider, within the bound.
No kernel may reach another device: no remote copies, remote signals or barrier semaphores. Data moves between devices by JAX's collectives and lax.ppermute only.
A program may use at most 192 MiB of HBM per device.

```python
import jax
import jax.numpy as jnp
from jax import lax

D = 1024
BLOCK = 128
BLK_DEV = 2
PAIRS = 384
GROUP = 64
CLUSTERS = 16
NBLK = 64
ROWS = 8192
N_DEV = 32


def cluster_bounds(key):
    base = jax.random.fold_in(key, 31)
    order = jax.random.permutation(jax.random.fold_in(base, 1), CLUSTERS).astype(jnp.int32)
    weights = jnp.int32(5040) // (order + 1)
    running = jnp.cumsum(weights).astype(jnp.int32)
    total = running[-1]
    bounds = running[:-1] * ROWS // total
    jitter = jax.random.randint(jax.random.fold_in(base, 2), (CLUSTERS - 1,), -(BLOCK // 4), BLOCK // 4 + 1).astype(jnp.int32)
    return (bounds + jitter).astype(jnp.int32)


def draw_cluster_id(key, part):
    bounds = cluster_bounds(key)
    rows_all = jnp.arange(ROWS, dtype=jnp.int32)
    return jnp.sum((rows_all[:, None] >= bounds[None, :]).astype(jnp.int32), axis=1).astype(jnp.int32)


def device_plan(key, device):
    width = min(N_DEV, 40)
    tri_left, tri_right = jnp.triu_indices(width)
    tri_left = tri_left.astype(jnp.int32)
    tri_right = tri_right.astype(jnp.int32)
    total = tri_left.shape[0]
    inner = jax.random.permutation(jax.random.fold_in(key, 1), total - 2)[:PAIRS - 2].astype(jnp.int32) + 1
    codes = jnp.concatenate([jnp.array([0, total - 1], dtype=jnp.int32), inner])
    codes = jax.random.permutation(jax.random.fold_in(key, 2), codes)
    drawn_start = jax.random.randint(jax.random.fold_in(key, 4), (), 0, N_DEV - width + 1).astype(jnp.int32)
    first_start = jnp.where(device == 0, jnp.int32(0), drawn_start)
    window_start = jnp.where(device == N_DEV - 1, jnp.int32(N_DEV - width), first_start)
    left = window_start + tri_left[codes]
    right = window_start + tri_right[codes]
    live = jnp.zeros((N_DEV,), jnp.int32).at[left].set(1).at[right].set(1)
    chosen = jax.random.randint(jax.random.fold_in(key, 3), (N_DEV,), 0, BLK_DEV).astype(jnp.int32)
    asks = jnp.where(live > 0, chosen, jnp.int32(-1))
    return (asks, left, right)


def whole_plan(key):
    base = jax.random.fold_in(key, 77)
    devices_all = jnp.arange(N_DEV, dtype=jnp.int32)
    keys = jax.vmap(lambda device: jax.random.fold_in(base, device))(devices_all)
    return jax.vmap(device_plan)(keys, devices_all)


def draw_requests(key, part):
    return whole_plan(key)[0].reshape(-1)


def draw_pair_left(key, part):
    return whole_plan(key)[1].reshape(-1)


def draw_pair_right(key, part):
    return whole_plan(key)[2].reshape(-1)


def levels(key, shape, split, low, top_value):
    factor_of, own = 1.0, jax.random.fold_in(key, 6)
    for axis_at, shards_of in split:
        heights = jnp.exp(jax.random.uniform(jax.random.fold_in(own, axis_at), (shards_of,), jnp.float32, low / len(split), top_value / len(split)))
        factor_of = factor_of * jnp.repeat(heights, shape[axis_at] // shards_of).reshape([-1 if axis == axis_at else 1 for axis in range(len(shape))])
    return factor_of


def bell_draw(own_key, dims, deviation, reach, pieces=(), kind=jnp.bfloat16):
    drawn = jax.random.normal(own_key, dims, jnp.float32) * deviation
    if len(pieces) > 0:
        drawn = levels(own_key, dims, pieces, -0.22, 0.18) * drawn
    return jnp.clip(drawn, min=-reach, max=reach).astype(kind)


def setup_inputs(seed: int = 0) -> dict:
    seeds = jax.random.split(jax.random.key(seed), 6)
    return {
        "embeddings": bell_draw(seeds[0], (ROWS, D), 1.0, 6.0, ((0, 32),)),
        "cluster_id": draw_cluster_id(jax.random.fold_in(seeds[5], 71), 0),
        "requests": draw_requests(jax.random.fold_in(seeds[5], 71), 0),
        "pair_left": draw_pair_left(jax.random.fold_in(seeds[5], 71), 0),
        "pair_right": draw_pair_right(jax.random.fold_in(seeds[5], 71), 0),
    }


def reference(embeddings, cluster_id, requests, pair_left, pair_right):
    values = embeddings.astype(jnp.float32)
    unit = (values * lax.rsqrt(lax.optimization_barrier(jnp.sum(values * values, axis=-1, keepdims=True)) + 1e-06)).astype(jnp.bfloat16)
    unit_blocks = unit.reshape(NBLK, BLOCK, D)
    labels = cluster_id.reshape(NBLK, BLOCK)
    table = requests.reshape(N_DEV, N_DEV)
    owners = jnp.repeat(jnp.arange(N_DEV, dtype=jnp.int32), PAIRS)
    block_left = (pair_left * BLK_DEV + table[owners, pair_left]).astype(jnp.int32)
    block_right = (pair_right * BLK_DEV + table[owners, pair_right]).astype(jnp.int32)
    diagonal_mask = jnp.eye(BLOCK, dtype=bool)

    def step(carry, indices):
        left, right = indices
        first = unit_blocks[left].astype(jnp.float32)
        second = unit_blocks[right].astype(jnp.float32)
        sims = jnp.einsum('gid,gjd->gij', first, second)
        same = labels[left][:, :, None] == labels[right][:, None, :]
        selfish = (left == right)[:, None, None] & diagonal_mask[None]
        sims = jnp.where(same & ~selfish, sims, jnp.float32(-1.0))
        carry = carry.at[left].max(lax.optimization_barrier(jnp.max(sims, axis=2)))
        carry = carry.at[right].max(lax.optimization_barrier(jnp.max(sims, axis=1)))
        return (carry, None)
    start = jnp.full((NBLK, BLOCK), -1.0, jnp.float32)
    result, _ = lax.scan(step, start, (block_left.reshape(-1, GROUP), block_right.reshape(-1, GROUP)))
    return result.reshape(ROWS)
```

```python
import functools

import jax
import jax.numpy as jnp
from jax import lax
from jax.experimental import pallas as pl
from jax.experimental.pallas import tpu as pltpu
from jax.sharding import PartitionSpec as P

BLOCK = 128
CLUSTERS = 16
PLANE = 8
AXIS = "dev"


def normalise_kernel(x_ref, unit_ref):
    values = x_ref[...].astype(jnp.float32)
    norm = lax.rsqrt(jnp.sum(values * values, axis=-1, keepdims=True) + 1e-06)
    unit_ref[...] = (values * norm).astype(jnp.bfloat16)


def normalise(x):
    return pl.pallas_call(
        normalise_kernel,
        out_shape=jax.ShapeDtypeStruct(x.shape, jnp.bfloat16),
        compiler_params=pltpu.CompilerParams(vmem_limit_bytes=16 * 1024 * 1024),
    )(x)


def tile_kernel(n_right, n_left, own_first, info_ref, *refs):
    rights, lefts, outs = refs[:n_right], refs[n_right : n_right + n_left], refs[n_right + n_left :]
    rows = rights[0].shape[0]

    def label_of(index):
        label = jnp.zeros(index.shape, jnp.int32)
        for c in range(1, CLUSTERS):
            label += (index >= info_ref[c]).astype(jnp.int32)
        return label

    lane = lax.broadcasted_iota(jnp.int32, (1, rows), 1)
    right_labels = [label_of(lane + info_ref[CLUSTERS + r]) for r in range(n_right)]
    for out in outs:
        out[...] = jnp.full(out.shape, -1.0, jnp.float32)
    for c in range(n_left):
        base = info_ref[CLUSTERS + n_right + c]
        index = lax.broadcasted_iota(jnp.int32, (rows, BLOCK), 0) + base
        label = jnp.where(base < 0, -1, label_of(index))
        label = jnp.concatenate([label] * (rows // BLOCK), axis=1)
        for r in range(n_right):
            sims = lax.dot_general(
                lefts[c][...], rights[r][...], (((1,), (1,)), ((), ())), preferred_element_type=jnp.float32
            )
            same = label == right_labels[r]
            if own_first and c == 0 and r == 0:
                same &= lax.broadcasted_iota(jnp.int32, sims.shape, 0) != lax.broadcasted_iota(
                    jnp.int32, sims.shape, 1
                )
            sims = jnp.where(same, sims, -1.0)
            for b in range(rows // BLOCK):
                at = c * (rows // BLOCK) + b
                outs[r][at : at + 1, :] = jnp.max(
                    sims[b * BLOCK : (b + 1) * BLOCK], axis=0, keepdims=True
                )


def tiles(rights, lefts, starts, right_bases, left_bases, own_first):
    rows, depth = rights[0].shape
    height = -(-len(lefts) * (rows // BLOCK) // 8) * 8
    info = jnp.concatenate([starts, jnp.stack(list(right_bases) + list(left_bases))]).astype(jnp.int32)
    n = len(rights) + len(lefts)
    return pl.pallas_call(
        functools.partial(tile_kernel, len(rights), len(lefts), own_first),
        in_specs=[pl.BlockSpec(memory_space=pltpu.SMEM)] + [pl.BlockSpec(memory_space=pltpu.VMEM)] * n,
        out_specs=[pl.BlockSpec(memory_space=pltpu.VMEM)] * len(rights),
        out_shape=[jax.ShapeDtypeStruct((height, rows), jnp.float32)] * len(rights),
        compiler_params=pltpu.CompilerParams(vmem_limit_bytes=32 * 1024 * 1024),
        cost_estimate=pl.CostEstimate(
            flops=2 * len(rights) * len(lefts) * rows * rows * depth,
            bytes_accessed=2 * n * rows * depth,
            transcendentals=0,
        ),
    )(info, *rights, *lefts)


def local(embeddings, cluster_id, requests, pair_left, pair_right):
    n = lax.axis_size(AXIS)
    me = lax.axis_index(AXIS)
    rows = embeddings.shape[0]
    blk_dev = rows // BLOCK
    n_planes = n // PLANE
    place, plane = me % PLANE, me // PLANE

    def swap(x, bit):
        return lax.ppermute(x, AXIS, [(i, i ^ bit) for i in range(n)])

    def from_above(x):
        return lax.ppermute(x, AXIS, [(i + PLANE, i) for i in range(n - PLANE)])

    def from_below(x):
        return lax.ppermute(x, AXIS, [(i, i + PLANE) for i in range(n - PLANE)])

    unit = normalise(embeddings)
    along_x, along_y = swap(unit, 2), swap(unit, 4)
    above, below = from_above(unit), from_below(unit)
    twin = swap(unit, 1)
    half = rows // 2
    across = jnp.concatenate([swap(along_x[:half], 4), swap(along_y[half:], 2)], axis=0)
    above_twin, below_twin = swap(above, 1), swap(below, 1)

    slots = jnp.arange(n, dtype=jnp.int32)
    left_hot = (slots[:, None] == pair_left[None, :]).astype(jnp.bfloat16)
    right_hot = (slots[:, None] == pair_right[None, :]).astype(jnp.bfloat16)
    listed = jnp.einsum("sp,tp->st", left_hot, right_hot, preferred_element_type=jnp.float32)
    listed = listed + listed.T
    counts = jnp.sum(
        (cluster_id[None, :] == jnp.arange(CLUSTERS, dtype=jnp.int32)[:, None]).astype(jnp.float32), axis=1
    )
    tail = jnp.concatenate([requests.astype(jnp.float32), counts])
    message = jnp.concatenate([listed, jnp.broadcast_to(tail[None], (n, tail.shape[0]))], axis=1)
    width = message.shape[1]
    message = jnp.pad(message, ((0, 0), (0, -width % BLOCK)))[:, None, :]
    heard = lax.all_to_all(message, AXIS, split_axis=0, concat_axis=0, tiled=True)[:, 0, :]
    heard_listed = heard[:, :n] > 0
    heard_requests = heard[:, n : 2 * n].astype(jnp.int32)
    counts = jnp.sum(heard[:, 2 * n : 2 * n + CLUSTERS], axis=0).astype(jnp.int32)
    ends = jnp.cumsum(counts)
    starts = ends - counts
    per_plane = rows * PLANE
    span = jnp.max(jnp.where(counts > 0, (ends - 1) // per_plane - starts // per_plane, 0))
    own_request = jnp.sum(jnp.where(slots[None, :] == me, heard_requests, 0), axis=1)
    blocks = jnp.arange(blk_dev, dtype=jnp.int32)
    covered = jnp.any(
        heard_listed[:, :, None, None]
        & (heard_requests[:, :, None, None] == blocks[None, None, :, None])
        & (own_request[:, None, None, None] == blocks[None, None, None, :]),
        axis=0,
    )
    covered = covered.reshape(n_planes, PLANE, blk_dev, blk_dev)
    covered = jnp.take(covered, jnp.arange(PLANE) ^ place, axis=1)
    caps = jnp.where(covered, jnp.float32(jnp.inf), jnp.float32(-1.0))
    caps = jnp.repeat(caps, BLOCK, axis=-1)
    caps = jnp.pad(caps, ((n_planes, n_planes), (0, 0), (0, 0), (0, 0)), constant_values=-1.0)

    def caps_of(offset):
        cap = lax.dynamic_index_in_dim(caps, plane + n_planes + offset, 0, keepdims=False)
        return cap.reshape(PLANE // 2, 2 * blk_dev, rows)

    def base_of(device, offset):
        at = plane + offset
        inside = (at >= 0) & (at < n_planes)
        return jnp.where(inside, (device + offset * PLANE) * rows, -1)

    right_bases = [(me ^ bit) * rows for bit in (0, 2, 4, 6)]

    lefts = [unit, twin, above, above_twin, below, below_twin]
    left_bases = [base_of(me ^ bit, offset) for offset in (0, 1, -1) for bit in (0, 1)]
    mine, for_x, for_y = tiles([unit, along_x, along_y], lefts, starts, right_bases[:3], left_bases, True)
    (for_across,) = tiles([across], lefts, starts, right_bases[3:], left_bases, False)
    near = jnp.stack([mine, swap(for_x, 2), swap(for_y, 4), swap(for_across, 6)])
    cap = jnp.concatenate([caps_of(0), caps_of(1), caps_of(-1)], axis=1)
    best = jnp.max(jnp.minimum(near[:, : cap.shape[1]], cap), axis=(0, 1))

    def further(best):
        def body(carry):
            offset, best, above, below = carry
            above, below = from_above(above), from_below(below)
            lefts = [above, swap(above, 1), below, swap(below, 1)]
            left_bases = [base_of(me ^ bit, o) for o in (offset, -offset) for bit in (0, 1)]
            mine, for_x, for_y, for_across = tiles(
                [unit, along_x, along_y, across], lefts, starts, right_bases, left_bases, False
            )
            far = jnp.stack([mine, swap(for_x, 2), swap(for_y, 4), swap(for_across, 6)])
            cap = jnp.concatenate([caps_of(offset), caps_of(-offset)], axis=1)
            best = jnp.maximum(best, jnp.max(jnp.minimum(far[:, : cap.shape[1]], cap), axis=(0, 1)))
            return offset + 1, best, above, below

        return lax.while_loop(lambda carry: carry[0] <= span, body, (jnp.int32(2), best, above, below))[1]

    best = lax.cond(span >= 2, further, lambda best: best, best)
    return jnp.maximum(best, -1.0)


def solution(mesh):
    in_specs = (P(AXIS, None), P(AXIS), P(AXIS), P(AXIS), P(AXIS))
    return jax.shard_map(local, mesh=mesh, in_specs=in_specs, out_specs=P(AXIS), check_vma=False)
```

```python
import functools

import jax
import jax.numpy as jnp
from jax import lax
from jax.experimental import pallas as pl
from jax.experimental.pallas import tpu as pltpu
from jax.sharding import PartitionSpec as P

BLOCK = 128
CLUSTERS = 16
PLANE = 8
LAST_COST = 10_000_000_000
JOIN_COST = 10_000_000_000
AXIS = "dev"
LABEL_ROWS = 16
VMEM_TILES = 8 * 1024 * 1024


def normalise_kernel(x_hbm, cluster_hbm, unit_ref, x_ref, cluster_ref, sems):
    copies = [
        pltpu.make_async_copy(x_hbm, x_ref, sems.at[0]),
        pltpu.make_async_copy(cluster_hbm, cluster_ref, sems.at[1]),
    ]
    for copy in copies:
        copy.start()
    rows, depth = x_ref.shape
    unit_ref[rows:] = jnp.zeros((LABEL_ROWS, depth), jnp.bfloat16)
    copies[1].wait()
    label = (cluster_ref[...] + 1).astype(jnp.bfloat16)
    unit_ref[rows:, :rows] = jnp.broadcast_to(label, (LABEL_ROWS, rows))
    copies[0].wait()
    values = x_ref[...].astype(jnp.float32)
    norm = lax.rsqrt(jnp.sum(values * values, axis=-1, keepdims=True) + 1e-06)
    unit_ref[:rows] = (values * norm).astype(jnp.bfloat16)


def normalise(x, cluster_id):
    rows, depth = x.shape
    return pl.pallas_call(
        normalise_kernel,
        in_specs=[pl.BlockSpec(memory_space=pltpu.HBM)] * 2,
        out_shape=jax.ShapeDtypeStruct((rows + LABEL_ROWS, depth), jnp.bfloat16),
        scratch_shapes=[
            pltpu.VMEM((rows, depth), x.dtype),
            pltpu.VMEM((1, rows), jnp.int32),
            pltpu.SemaphoreType.DMA((2,)),
        ],
        compiler_params=pltpu.CompilerParams(vmem_limit_bytes=60 * 1024 * 1024),
    )(x, cluster_id.reshape(1, rows))


def message_kernel(n, left_ref, right_ref, request_ref, cluster_ref, out_ref):
    def dot(a, b):
        return lax.dot_general(a, b, (((1,), (1,)), ((), ())), preferred_element_type=jnp.float32)

    def hot(count, ref):
        index = lax.broadcasted_iota(jnp.int32, (count, ref.shape[1]), 0)
        return (index == ref[...]).astype(jnp.float32).astype(jnp.bfloat16)

    left, right, cluster = hot(n, left_ref), hot(n, right_ref), hot(CLUSTERS, cluster_ref)
    out_ref[...] = jnp.zeros(out_ref.shape, jnp.float32)
    out_ref[:, 0, :n] = dot(left, right) + dot(right, left)
    out_ref[:, 0, n : 2 * n] = jnp.broadcast_to(request_ref[...].astype(jnp.float32), (n, n))
    counts = dot(jnp.ones((n, cluster.shape[1]), jnp.bfloat16), cluster)
    out_ref[:, 0, 2 * n : 2 * n + CLUSTERS] = counts


def message_of(requests, pair_left, pair_right, cluster_id):
    n = requests.shape[0]
    width = -(-(2 * n + CLUSTERS) // BLOCK) * BLOCK
    return pl.pallas_call(
        functools.partial(message_kernel, n),
        out_shape=jax.ShapeDtypeStruct((n, 1, width), jnp.float32),
        compiler_params=pltpu.CompilerParams(vmem_limit_bytes=4 * 1024 * 1024),
    )(pair_left.reshape(1, -1), pair_right.reshape(1, -1), requests.reshape(1, -1), cluster_id.reshape(1, -1))


def halves_kernel(x_ref, y_ref, first_ref, second_ref):
    first_ref[...] = x_ref[: first_ref.shape[0]]
    second_ref[...] = y_ref[first_ref.shape[0] :]


def halves(x, y):
    half = (x.shape[0] - LABEL_ROWS) // 2
    return pl.pallas_call(
        halves_kernel,
        out_shape=[
            jax.ShapeDtypeStruct((half, x.shape[1]), x.dtype),
            jax.ShapeDtypeStruct((half + LABEL_ROWS, x.shape[1]), x.dtype),
        ],
        compiler_params=pltpu.CompilerParams(vmem_limit_bytes=4 * 1024 * 1024),
        cost_estimate=pl.CostEstimate(flops=0, bytes_accessed=x.size * 4, transcendentals=0),
    )(x, y)


def join_kernel(first_ref, second_ref, x_ref):
    x_ref[: first_ref.shape[0]] = first_ref[...]
    x_ref[first_ref.shape[0] :] = second_ref[...]


def join(first, second):
    return pl.pallas_call(
        join_kernel,
        out_shape=jax.ShapeDtypeStruct((first.shape[0] + second.shape[0], first.shape[1]), first.dtype),
        compiler_params=pltpu.CompilerParams(vmem_limit_bytes=4 * 1024 * 1024),
        cost_estimate=pl.CostEstimate(flops=JOIN_COST, bytes_accessed=first.size * 8, transcendentals=0),
    )(first, second)


def tile_kernel(n_right, places, rows, own_first, n_before, *refs):
    right_refs, refs = refs[:n_right], refs[n_right:]
    left_refs, refs = refs[: len(places)], refs[len(places) :]
    before, outs = refs[: n_before], refs[n_before :]
    right_rows = [right[:rows] for right in right_refs]
    right_labels = [right[rows:, :rows].astype(jnp.float32)[:1] for right in right_refs]
    for r, out in enumerate(outs):
        out[...] = jnp.full(out.shape, -1.0, jnp.float32)
        if r < n_before:
            out[: before[r].shape[0]] = before[r][...]
    blocks = rows // BLOCK
    for c, left in enumerate(left_refs):
        left_label = left[rows:, :rows].astype(jnp.float32)[:1]
        for r, out in enumerate(outs):
            if r < n_before and places[c] < before[r].shape[0]:
                continue
            sims = lax.dot_general(
                left[:rows], right_rows[r], (((1,), (1,)), ((), ())), preferred_element_type=jnp.float32
            )
            for b in range(blocks):
                at = slice(b * BLOCK, (b + 1) * BLOCK)
                label = jnp.broadcast_to(left_label[:, at], (BLOCK, BLOCK)).T
                label = jnp.concatenate([label] * blocks, axis=1)
                same = label == right_labels[r]
                part = sims[at]
                if own_first and c == 0 and r == 0:
                    index = lax.broadcasted_iota(jnp.int32, part.shape, 0) + b * BLOCK
                    same &= index != lax.broadcasted_iota(jnp.int32, part.shape, 1)
                part = jnp.where(same, part, -1.0)
                row = places[c] + b
                out[row : row + 1, :] = jnp.max(part, axis=0, keepdims=True)


def tiles(rights, lefts, places, own_first, before=(), flops=None):
    rows, depth = lefts[0].shape
    rows -= LABEL_ROWS
    height = -(-(places[-1] + rows // BLOCK) // 8) * 8
    if flops is None:
        flops = 2 * len(rights) * len(lefts) * rows * rows * depth
    operands = list(rights) + list(lefts) + list(before)
    return pl.pallas_call(
        functools.partial(tile_kernel, len(rights), tuple(places), rows, own_first, len(before)),
        in_specs=[pl.BlockSpec(memory_space=pltpu.VMEM)] * len(operands),
        out_specs=[pl.BlockSpec(memory_space=pltpu.VMEM)] * len(rights),
        out_shape=[jax.ShapeDtypeStruct((height, rows), jnp.float32)] * len(rights),
        compiler_params=pltpu.CompilerParams(vmem_limit_bytes=VMEM_TILES),
        cost_estimate=pl.CostEstimate(
            flops=flops, bytes_accessed=2 * len(operands) * rows * depth, transcendentals=0
        ),
    )(*operands)


def local(embeddings, cluster_id, requests, pair_left, pair_right):
    n = lax.axis_size(AXIS)
    me = lax.axis_index(AXIS)
    rows = embeddings.shape[0]
    blk_dev = rows // BLOCK
    n_planes = n // PLANE
    place, plane = me % PLANE, me // PLANE

    def swap(x, bit):
        return lax.ppermute(x, AXIS, [(i, i ^ bit) for i in range(n)])

    def from_above(x):
        return lax.ppermute(x, AXIS, [(i + PLANE, i) for i in range(n - PLANE)])

    def from_below(x):
        return lax.ppermute(x, AXIS, [(i, i + PLANE) for i in range(n - PLANE)])

    unit = normalise(embeddings, cluster_id)
    along_x, along_y = swap(unit, 2), swap(unit, 4)
    above, below = from_above(unit), from_below(unit)
    twin = swap(unit, 1)
    first, second = halves(along_x, along_y)
    pieces = [swap(first, 4), swap(second, 2)]
    along_x, first = lax.optimization_barrier((along_x, first))
    near_rights = [unit, along_x, along_y]
    plane_places = [0, blk_dev]
    next_places = [8 + blk_dev * k for k in range(4)]
    plane_parts = list(tiles(near_rights, [unit, twin], plane_places, True))
    above_twin, below_twin = swap(above, 1), swap(below, 1)

    slots = jnp.arange(n, dtype=jnp.int32)
    message = message_of(requests, pair_left, pair_right, cluster_id)
    heard = lax.all_to_all(message, AXIS, split_axis=0, concat_axis=0, tiled=True)[:, 0, :]
    lefts = [above, above_twin, below, below_twin]
    mine, for_x, for_y = tiles(near_rights, lefts, next_places, False, plane_parts)
    across = join(*pieces)
    (for_across,) = tiles([across], [unit, twin] + lefts, plane_places + next_places, False, flops=LAST_COST)
    heard, mine = lax.optimization_barrier((heard, mine))
    near = jnp.stack([mine, swap(for_x, 2), swap(for_y, 4), swap(for_across, 6)])
    heard_listed = heard[:, :n] > 0
    heard_requests = heard[:, n : 2 * n].astype(jnp.int32)
    counts = jnp.sum(heard[:, 2 * n : 2 * n + CLUSTERS], axis=0).astype(jnp.int32)
    ends = jnp.cumsum(counts)
    starts = ends - counts
    per_plane = rows * PLANE
    span = jnp.max(jnp.where(counts > 0, (ends - 1) // per_plane - starts // per_plane, 0))
    own_request = jnp.sum(jnp.where(slots[None, :] == me, heard_requests, 0), axis=1)
    blocks = jnp.arange(blk_dev, dtype=jnp.int32)
    covered = jnp.any(
        heard_listed[:, :, None, None]
        & (heard_requests[:, :, None, None] == blocks[None, None, :, None])
        & (own_request[:, None, None, None] == blocks[None, None, None, :]),
        axis=0,
    )
    covered = covered.reshape(n_planes, PLANE, blk_dev, blk_dev)
    covered = jnp.take(covered, jnp.arange(PLANE) ^ place, axis=1)
    caps = jnp.where(covered, jnp.float32(jnp.inf), jnp.float32(-1.0))
    caps = jnp.repeat(caps, BLOCK, axis=-1)
    caps = jnp.pad(caps, ((n_planes, n_planes), (0, 0), (0, 0), (0, 0)), constant_values=-1.0)

    def caps_of(offset):
        cap = lax.dynamic_index_in_dim(caps, plane + n_planes + offset, 0, keepdims=False)
        return cap.reshape(PLANE // 2, 2 * blk_dev, rows)

    cap = jnp.pad(caps_of(0), ((0, 0), (0, 8 - 2 * blk_dev), (0, 0)), constant_values=-1.0)
    cap = jnp.concatenate([cap, caps_of(1), caps_of(-1)], axis=1)
    best = jnp.max(jnp.minimum(near, cap), axis=(0, 1))

    def further(best):
        def body(carry):
            offset, best, above, below = carry
            above, below = from_above(above), from_below(below)
            lefts = [above, swap(above, 1), below, swap(below, 1)]
            mine, for_x, for_y, for_across = tiles(
                near_rights + [across], lefts, [blk_dev * k for k in range(4)], False
            )
            far = jnp.stack([mine, swap(for_x, 2), swap(for_y, 4), swap(for_across, 6)])
            cap = jnp.concatenate([caps_of(offset), caps_of(-offset)], axis=1)
            best = jnp.maximum(best, jnp.max(jnp.minimum(far[:, : cap.shape[1]], cap), axis=(0, 1)))
            return offset + 1, best, above, below

        return lax.while_loop(lambda carry: carry[0] <= span, body, (jnp.int32(2), best, above, below))[1]

    best = lax.cond(span >= 2, further, lambda best: best, best)
    return jnp.maximum(best, -1.0)


def solution(mesh):
    in_specs = (P(AXIS, None), P(AXIS), P(AXIS), P(AXIS), P(AXIS))
    return jax.shard_map(local, mesh=mesh, in_specs=in_specs, out_specs=P(AXIS), check_vma=False)
```

```python
import functools

import jax
import jax.numpy as jnp
from jax import lax
from jax.experimental import pallas as pl
from jax.experimental.pallas import tpu as pltpu
from jax.sharding import PartitionSpec as P

BLOCK = 128
CLUSTERS = 16
PLANE = 8
JOIN_COST = 10_000_000_000
AXIS = "dev"
LABEL_ROWS = 16
VMEM_TILES = 8 * 1024 * 1024


def normalise_kernel(x_hbm, cluster_hbm, unit_ref, x_ref, cluster_ref, sems):
    copies = [
        pltpu.make_async_copy(x_hbm, x_ref, sems.at[0]),
        pltpu.make_async_copy(cluster_hbm, cluster_ref, sems.at[1]),
    ]
    for copy in copies:
        copy.start()
    rows, depth = x_ref.shape
    unit_ref[rows:] = jnp.zeros((LABEL_ROWS, depth), jnp.bfloat16)
    copies[1].wait()
    label = (cluster_ref[...] + 1).astype(jnp.bfloat16)
    unit_ref[rows:, :rows] = jnp.broadcast_to(label, (LABEL_ROWS, rows))
    copies[0].wait()
    values = x_ref[...].astype(jnp.float32)
    norm = lax.rsqrt(jnp.sum(values * values, axis=-1, keepdims=True) + 1e-06)
    unit_ref[:rows] = (values * norm).astype(jnp.bfloat16)


def normalise(x, cluster_id):
    rows, depth = x.shape
    return pl.pallas_call(
        normalise_kernel,
        name="normalise",
        in_specs=[pl.BlockSpec(memory_space=pltpu.HBM)] * 2,
        out_shape=jax.ShapeDtypeStruct((rows + LABEL_ROWS, depth), jnp.bfloat16),
        scratch_shapes=[
            pltpu.VMEM((rows, depth), x.dtype),
            pltpu.VMEM((1, rows), jnp.int32),
            pltpu.SemaphoreType.DMA((2,)),
        ],
        compiler_params=pltpu.CompilerParams(vmem_limit_bytes=60 * 1024 * 1024),
    )(x, cluster_id.reshape(1, rows))


def message_kernel(n, left_ref, right_ref, request_ref, cluster_ref, out_ref):
    def dot(a, b):
        return lax.dot_general(a, b, (((1,), (1,)), ((), ())), preferred_element_type=jnp.float32)

    def hot(count, ref):
        index = lax.broadcasted_iota(jnp.int32, (count, ref.shape[1]), 0)
        return (index == ref[...]).astype(jnp.float32).astype(jnp.bfloat16)

    left, right, cluster = hot(n, left_ref), hot(n, right_ref), hot(CLUSTERS, cluster_ref)
    out_ref[...] = jnp.zeros(out_ref.shape, jnp.float32)
    out_ref[:, 0, :n] = dot(left, right) + dot(right, left)
    out_ref[:, 0, n : 2 * n] = jnp.broadcast_to(request_ref[...].astype(jnp.float32), (n, n))
    counts = dot(jnp.ones((n, cluster.shape[1]), jnp.bfloat16), cluster)
    out_ref[:, 0, 2 * n : 2 * n + CLUSTERS] = counts


def message_of(requests, pair_left, pair_right, cluster_id):
    n = requests.shape[0]
    width = -(-(2 * n + CLUSTERS) // BLOCK) * BLOCK
    return pl.pallas_call(
        functools.partial(message_kernel, n),
        name="message",
        out_shape=jax.ShapeDtypeStruct((n, 1, width), jnp.float32),
        compiler_params=pltpu.CompilerParams(vmem_limit_bytes=4 * 1024 * 1024),
    )(pair_left.reshape(1, -1), pair_right.reshape(1, -1), requests.reshape(1, -1), cluster_id.reshape(1, -1))


def cover_kernel(blk_dev, rows, offset_ref, heard_ref, cap_ref, span_ref):
    n = heard_ref.shape[0]
    me = lax.axis_index(AXIS)

    def iota(shape, dimension):
        return lax.broadcasted_iota(jnp.int32, shape, dimension)

    def hot(mask):
        return mask.astype(jnp.float32)

    listed = heard_ref[:, 0, :n] > 0
    requests = heard_ref[:, 0, n : 2 * n]
    own = jnp.sum(jnp.where(iota((n, n), 1) == me, requests, 0.0), axis=1, keepdims=True)
    owns = hot(own == (iota((n, rows), 1) // BLOCK).astype(jnp.float32)).astype(jnp.bfloat16)
    height = cap_ref.shape[1]
    at = iota((4 * height, n), 0)
    source, at = at // height, at % height
    near = at < 8
    at = jnp.where(near, at, at - 8)
    part, block = at // blk_dev, at % blk_dev
    step = jnp.where(near, 0, jnp.where(part < 2, offset_ref[0], -offset_ref[0]))
    device = ((2 * source + part % 2) ^ me) + step * PLANE
    device = jnp.where(near & (part >= 2), -1, device)
    total = jnp.zeros((4 * height, rows), jnp.float32)
    for b in range(blk_dev):
        asked = hot(listed & (requests == b)).T.astype(jnp.bfloat16)
        count = jnp.dot(asked, owns, preferred_element_type=jnp.float32)
        pick = hot((iota((4 * height, n), 1) == device) & (block == b)).astype(jnp.bfloat16)
        total += jnp.dot(pick, hot(count > 0).astype(jnp.bfloat16), preferred_element_type=jnp.float32)
    cap_ref[...] = jnp.where(total > 0, jnp.inf, -1.0).reshape(cap_ref.shape)
    present = heard_ref[:, 0, 2 * n : 2 * n + CLUSTERS] > 0
    plane = (iota((n, CLUSTERS), 0) // PLANE).astype(jnp.float32)
    first = jnp.min(jnp.where(present, plane, float(n)), axis=0, keepdims=True)
    last = jnp.max(jnp.where(present, plane, -1.0), axis=0, keepdims=True)
    span_ref[0] = jnp.max(last - first).astype(jnp.int32)


def cover(heard, offset, blk_dev, rows):
    cap, span = pl.pallas_call(
        functools.partial(cover_kernel, blk_dev, rows),
        name="cover",
        in_specs=[pl.BlockSpec(memory_space=pltpu.SMEM), pl.BlockSpec(memory_space=pltpu.VMEM)],
        out_specs=[pl.BlockSpec(memory_space=pltpu.VMEM), pl.BlockSpec(memory_space=pltpu.SMEM)],
        out_shape=[
            jax.ShapeDtypeStruct((4, 8 + 4 * blk_dev, rows), jnp.float32),
            jax.ShapeDtypeStruct((1,), jnp.int32),
        ],
        compiler_params=pltpu.CompilerParams(vmem_limit_bytes=8 * 1024 * 1024),
    )(jnp.asarray(offset, jnp.int32).reshape(1), heard)
    return cap, span[0]


def halves_kernel(x_ref, y_ref, first_ref, second_ref):
    first_ref[...] = x_ref[: first_ref.shape[0]]
    second_ref[...] = y_ref[first_ref.shape[0] :]


def halves(x, y):
    half = (x.shape[0] - LABEL_ROWS) // 2
    return pl.pallas_call(
        halves_kernel,
        name="halves",
        out_shape=[
            jax.ShapeDtypeStruct((half, x.shape[1]), x.dtype),
            jax.ShapeDtypeStruct((half + LABEL_ROWS, x.shape[1]), x.dtype),
        ],
        compiler_params=pltpu.CompilerParams(vmem_limit_bytes=4 * 1024 * 1024),
        cost_estimate=pl.CostEstimate(flops=0, bytes_accessed=x.size * 4, transcendentals=0),
    )(x, y)


def join_kernel(first_ref, second_ref, x_ref):
    x_ref[: first_ref.shape[0]] = first_ref[...]
    x_ref[first_ref.shape[0] :] = second_ref[...]


def join(first, second):
    return pl.pallas_call(
        join_kernel,
        name="join",
        out_shape=jax.ShapeDtypeStruct((first.shape[0] + second.shape[0], first.shape[1]), first.dtype),
        compiler_params=pltpu.CompilerParams(vmem_limit_bytes=4 * 1024 * 1024),
        cost_estimate=pl.CostEstimate(flops=JOIN_COST, bytes_accessed=first.size * 8, transcendentals=0),
    )(first, second)


def tile_kernel(pieces, places, rows, own_first, n_before, *refs):
    n_right = len(pieces)
    right_refs, refs = refs[: sum(pieces)], refs[sum(pieces) :]
    left_refs, refs = refs[: len(places)], refs[len(places) :]
    before, refs = refs[:n_before], refs[n_before:]
    outs, joined = refs[:n_right], refs[n_right:]

    def label_of(ref):
        label = ref[ref.shape[0] - LABEL_ROWS :, :rows].astype(jnp.float32)[:1]
        return label, jnp.min(label), jnp.max(label)

    rights, right_labels = [], []
    for count in pieces:
        part, right_refs = right_refs[:count], right_refs[count:]
        right_labels.append(label_of(part[-1]))
        if count > 1:
            half = part[0].shape[0]
            joined[0][:half] = part[0][...]
            joined[0][half:rows] = part[1][: rows - half]
            part, joined = joined[:1], joined[1:]
        rights.append(part[0])
    for r, out in enumerate(outs):
        out[...] = jnp.full(out.shape, -1.0, jnp.float32)
        if r < n_before:
            out[: before[r].shape[0]] = before[r][...]
    blocks = rows // BLOCK
    left_labels = [label_of(left) for left in left_refs]

    def tile(r, c):
        sims = lax.dot_general(
            left_refs[c][:rows], rights[r][:rows], (((1,), (1,)), ((), ())), preferred_element_type=jnp.float32
        )
        for b in range(blocks):
            at = slice(b * BLOCK, (b + 1) * BLOCK)
            label = jnp.broadcast_to(left_labels[c][0][:, at], (BLOCK, BLOCK)).T
            label = jnp.concatenate([label] * blocks, axis=1)
            same = label == right_labels[r][0]
            part = sims[at]
            if own_first and c == 0 and r == 0:
                index = lax.broadcasted_iota(jnp.int32, part.shape, 0) + b * BLOCK
                same &= index != lax.broadcasted_iota(jnp.int32, part.shape, 1)
            part = jnp.where(same, part, -1.0)
            row = places[c] + b
            outs[r][row : row + 1, :] = jnp.max(part, axis=0, keepdims=True)

    for c in range(len(places)):
        for r in range(n_right):
            if r < n_before and places[c] < before[r].shape[0]:
                continue
            meet = (left_labels[c][1] <= right_labels[r][2]) & (right_labels[r][1] <= left_labels[c][2])
            pl.when(meet)(functools.partial(tile, r, c))


def tiles(name, rights, lefts, places, own_first, before=(), flops=None):
    rows, depth = lefts[0].shape
    rows -= LABEL_ROWS
    height = -(-(places[-1] + rows // BLOCK) // 8) * 8
    if flops is None:
        flops = 2 * len(rights) * len(lefts) * rows * rows * depth
    pieces = tuple(len(part) for part in rights)
    operands = [piece for part in rights for piece in part] + list(lefts) + list(before)
    return pl.pallas_call(
        functools.partial(tile_kernel, pieces, tuple(places), rows, own_first, len(before)),
        name=name,
        in_specs=[pl.BlockSpec(memory_space=pltpu.VMEM)] * len(operands),
        out_specs=[pl.BlockSpec(memory_space=pltpu.VMEM)] * len(rights),
        out_shape=[jax.ShapeDtypeStruct((height, rows), jnp.float32)] * len(rights),
        scratch_shapes=[pltpu.VMEM((rows, depth), jnp.bfloat16) for count in pieces if count > 1],
        compiler_params=pltpu.CompilerParams(vmem_limit_bytes=VMEM_TILES),
        cost_estimate=pl.CostEstimate(
            flops=flops, bytes_accessed=2 * len(operands) * rows * depth, transcendentals=0
        ),
    )(*operands)


def local(embeddings, cluster_id, requests, pair_left, pair_right):
    n = lax.axis_size(AXIS)
    rows = embeddings.shape[0]
    blk_dev = rows // BLOCK

    def swap(x, bit):
        return lax.ppermute(x, AXIS, [(i, i ^ bit) for i in range(n)])

    def from_above(x):
        return lax.ppermute(x, AXIS, [(i + PLANE, i) for i in range(n - PLANE)])

    def from_below(x):
        return lax.ppermute(x, AXIS, [(i, i + PLANE) for i in range(n - PLANE)])

    def owners_best(parts, cap):
        mine, for_x, for_y, for_across = parts
        returned = jnp.stack([mine, swap(for_x, 2), swap(for_y, 4), swap(for_across, 6)])
        return jnp.max(jnp.minimum(returned, cap), axis=(0, 1))

    unit = normalise(embeddings, cluster_id)
    along_x, along_y = swap(unit, 2), swap(unit, 4)
    above, below = from_above(unit), from_below(unit)
    twin = swap(unit, 1)
    first, second = halves(along_x, along_y)
    pieces = [swap(first, 4), swap(second, 2)]
    along_x, first = lax.optimization_barrier((along_x, first))
    above_twin, below_twin = swap(above, 1), swap(below, 1)

    message = message_of(requests, pair_left, pair_right, cluster_id)
    heard = lax.all_to_all(message, AXIS, split_axis=0, concat_axis=0, tiled=True)

    plane_places = [0, blk_dev]
    next_places = [8 + blk_dev * k for k in range(4)]
    lefts = [above, above_twin, below, below_twin]
    near_rights = [[unit], [along_x], [along_y]]
    plane_parts = tiles("plane_tiles", near_rights, [unit, twin], plane_places, True)
    across = join(*pieces)
    parts = tiles(
        "all_tiles",
        near_rights + [[across]],
        [unit, twin] + lefts,
        plane_places + next_places,
        False,
        plane_parts,
        flops=0,
    )
    cap, span = cover(heard, 1, blk_dev, rows)
    best = owners_best(parts, cap)

    def further(best):
        def body(carry):
            offset, best, above, below = carry
            above, below = from_above(above), from_below(below)
            lefts = [above, swap(above, 1), below, swap(below, 1)]
            parts = tiles(
                "further_tiles",
                near_rights + [[join(*pieces)]],
                lefts,
                [blk_dev * k for k in range(4)],
                False,
            )
            cap, _ = cover(heard, offset, blk_dev, rows)
            best = jnp.maximum(best, owners_best(parts, cap[:, 8:]))
            return offset + 1, best, above, below

        return lax.while_loop(lambda carry: carry[0] <= span, body, (jnp.int32(2), best, above, below))[1]

    best = lax.cond(span >= 2, further, lambda best: best, best)
    return jnp.maximum(best, -1.0)


def solution(mesh):
    in_specs = (P(AXIS, None), P(AXIS), P(AXIS), P(AXIS), P(AXIS))
    return jax.shard_map(local, mesh=mesh, in_specs=in_specs, out_specs=P(AXIS), check_vma=False)
```

```python
import functools

import jax
import jax.numpy as jnp
from jax import lax
from jax.experimental import pallas as pl
from jax.experimental.pallas import tpu as pltpu
from jax.sharding import PartitionSpec as P

BLOCK = 128
CLUSTERS = 16
PLANE = 8
JOIN_COST = 10_000_000_000
AXIS = "dev"
LABEL_ROWS = 16
VMEM_TILES = 8 * 1024 * 1024


def normalise_kernel(x_hbm, cluster_hbm, unit_ref, x_ref, cluster_ref, sems):
    copies = [
        pltpu.make_async_copy(x_hbm, x_ref, sems.at[0]),
        pltpu.make_async_copy(cluster_hbm, cluster_ref, sems.at[1]),
    ]
    for copy in copies:
        copy.start()
    rows, depth = x_ref.shape
    unit_ref[rows:] = jnp.zeros((LABEL_ROWS, depth), jnp.bfloat16)
    copies[1].wait()
    label = (cluster_ref[...] + 1).astype(jnp.bfloat16)
    unit_ref[rows:, :rows] = jnp.broadcast_to(label, (LABEL_ROWS, rows))
    copies[0].wait()
    values = x_ref[...].astype(jnp.float32)
    norm = lax.rsqrt(jnp.sum(values * values, axis=-1, keepdims=True) + 1e-06)
    unit_ref[:rows] = (values * norm).astype(jnp.bfloat16)


def normalise(x, cluster_id):
    rows, depth = x.shape
    return pl.pallas_call(
        normalise_kernel,
        name="normalise",
        in_specs=[pl.BlockSpec(memory_space=pltpu.HBM)] * 2,
        out_shape=jax.ShapeDtypeStruct((rows + LABEL_ROWS, depth), jnp.bfloat16),
        scratch_shapes=[
            pltpu.VMEM((rows, depth), x.dtype),
            pltpu.VMEM((1, rows), jnp.int32),
            pltpu.SemaphoreType.DMA((2,)),
        ],
        compiler_params=pltpu.CompilerParams(vmem_limit_bytes=60 * 1024 * 1024),
    )(x, cluster_id.reshape(1, rows))


def message_kernel(n, left_ref, right_ref, request_ref, cluster_ref, out_ref):
    def dot(a, b):
        return lax.dot_general(a, b, (((1,), (1,)), ((), ())), preferred_element_type=jnp.float32)

    def hot(count, ref):
        index = lax.broadcasted_iota(jnp.int32, (count, ref.shape[1]), 0)
        return (index == ref[...]).astype(jnp.float32).astype(jnp.bfloat16)

    left, right, cluster = hot(n, left_ref), hot(n, right_ref), hot(CLUSTERS, cluster_ref)
    out_ref[...] = jnp.zeros(out_ref.shape, jnp.float32)
    out_ref[:, 0, :n] = dot(left, right) + dot(right, left)
    out_ref[:, 0, n : 2 * n] = jnp.broadcast_to(request_ref[...].astype(jnp.float32), (n, n))
    counts = dot(jnp.ones((n, cluster.shape[1]), jnp.bfloat16), cluster)
    out_ref[:, 0, 2 * n : 2 * n + CLUSTERS] = counts


def message_of(requests, pair_left, pair_right, cluster_id):
    n = requests.shape[0]
    width = -(-(2 * n + CLUSTERS) // BLOCK) * BLOCK
    return pl.pallas_call(
        functools.partial(message_kernel, n),
        name="message",
        out_shape=jax.ShapeDtypeStruct((n, 1, width), jnp.float32),
        compiler_params=pltpu.CompilerParams(vmem_limit_bytes=4 * 1024 * 1024),
    )(pair_left.reshape(1, -1), pair_right.reshape(1, -1), requests.reshape(1, -1), cluster_id.reshape(1, -1))


def cover_kernel(blk_dev, rows, offset_ref, heard_ref, cap_ref, span_ref):
    n = heard_ref.shape[0]
    me = lax.axis_index(AXIS)

    def iota(shape, dimension):
        return lax.broadcasted_iota(jnp.int32, shape, dimension)

    def hot(mask):
        return mask.astype(jnp.float32)

    listed = heard_ref[:, 0, :n] > 0
    requests = heard_ref[:, 0, n : 2 * n]
    own = jnp.sum(jnp.where(iota((n, n), 1) == me, requests, 0.0), axis=1, keepdims=True)
    owns = hot(own == (iota((n, rows), 1) // BLOCK).astype(jnp.float32)).astype(jnp.bfloat16)
    height = cap_ref.shape[1]
    at = iota((4 * height, n), 0)
    source, at = at // height, at % height
    near = at < 8
    at = jnp.where(near, at, at - 8)
    part, block = at // blk_dev, at % blk_dev
    step = jnp.where(near, 0, jnp.where(part < 2, offset_ref[0], -offset_ref[0]))
    device = ((2 * source + part % 2) ^ me) + step * PLANE
    device = jnp.where(near & (part >= 2), -1, device)
    total = jnp.zeros((4 * height, rows), jnp.float32)
    for b in range(blk_dev):
        asked = hot(listed & (requests == b)).T.astype(jnp.bfloat16)
        count = jnp.dot(asked, owns, preferred_element_type=jnp.float32)
        pick = hot((iota((4 * height, n), 1) == device) & (block == b)).astype(jnp.bfloat16)
        total += jnp.dot(pick, hot(count > 0).astype(jnp.bfloat16), preferred_element_type=jnp.float32)
    cap_ref[...] = jnp.where(total > 0, jnp.inf, -1.0).reshape(cap_ref.shape)
    present = heard_ref[:, 0, 2 * n : 2 * n + CLUSTERS] > 0
    plane = (iota((n, CLUSTERS), 0) // PLANE).astype(jnp.float32)
    first = jnp.min(jnp.where(present, plane, float(n)), axis=0, keepdims=True)
    last = jnp.max(jnp.where(present, plane, -1.0), axis=0, keepdims=True)
    span_ref[0] = jnp.max(last - first).astype(jnp.int32)


def cover(heard, offset, blk_dev, rows):
    cap, span = pl.pallas_call(
        functools.partial(cover_kernel, blk_dev, rows),
        name="cover",
        in_specs=[pl.BlockSpec(memory_space=pltpu.SMEM), pl.BlockSpec(memory_space=pltpu.VMEM)],
        out_specs=[pl.BlockSpec(memory_space=pltpu.VMEM), pl.BlockSpec(memory_space=pltpu.SMEM)],
        out_shape=[
            jax.ShapeDtypeStruct((4, 8 + 4 * blk_dev, rows), jnp.float32),
            jax.ShapeDtypeStruct((1,), jnp.int32),
        ],
        compiler_params=pltpu.CompilerParams(vmem_limit_bytes=8 * 1024 * 1024),
    )(jnp.asarray(offset, jnp.int32).reshape(1), heard)
    return cap, span[0]


def halves_kernel(x_ref, y_ref, first_ref, second_ref):
    first_ref[...] = x_ref[: first_ref.shape[0]]
    second_ref[...] = y_ref[first_ref.shape[0] :]


def halves(x, y):
    half = (x.shape[0] - LABEL_ROWS) // 2
    return pl.pallas_call(
        halves_kernel,
        name="halves",
        out_shape=[
            jax.ShapeDtypeStruct((half, x.shape[1]), x.dtype),
            jax.ShapeDtypeStruct((half + LABEL_ROWS, x.shape[1]), x.dtype),
        ],
        compiler_params=pltpu.CompilerParams(vmem_limit_bytes=4 * 1024 * 1024),
        cost_estimate=pl.CostEstimate(flops=0, bytes_accessed=x.size * 4, transcendentals=0),
    )(x, y)


def arrived_kernel(first_ref, second_ref, token_ref):
    del first_ref, second_ref
    token_ref[...] = jnp.zeros(token_ref.shape, jnp.float32)


def arrived(pieces):
    return pl.pallas_call(
        arrived_kernel,
        name="arrived",
        in_specs=[pl.BlockSpec(memory_space=pl.ANY)] * 2,
        out_shape=jax.ShapeDtypeStruct((8, 128), jnp.float32),
        compiler_params=pltpu.CompilerParams(vmem_limit_bytes=1024 * 1024),
        cost_estimate=pl.CostEstimate(flops=JOIN_COST, bytes_accessed=4096, transcendentals=0),
    )(*pieces)


def tile_kernel(counts, n_right, places, rows, own_first, n_before, n_token, *refs):
    parts, copies = [], []
    n_operands = sum(max(count, 1) for count in counts)
    tail = refs[n_operands + n_before + n_token :]
    outs, scratch = tail[:n_right], tail[n_right:]
    operands, before = list(refs[:n_operands]), refs[n_operands : n_operands + n_before]
    sem = 0
    for count in counts:
        here, operands = operands[: max(count, 1)], operands[max(count, 1) :]
        if not count:
            parts.append(here[0])
            copies.append([])
            continue
        part, top, own = scratch[sum(1 for c in copies if c)], 0, []
        for piece in here:
            own.append(pltpu.make_async_copy(piece, part.at[pl.ds(top, piece.shape[0])], scratch[-1].at[sem]))
            own[-1].start()
            top, sem = top + piece.shape[0], sem + 1
        parts.append(part)
        copies.append(own)
    for r, out in enumerate(outs):
        out[...] = jnp.full(out.shape, -1.0, jnp.float32)
        if r < n_before:
            out[: before[r].shape[0]] = before[r][...]
    blocks = rows // BLOCK
    labels = {}

    def labels_of(k):
        if k not in labels:
            for copy in copies[k]:
                copy.wait()
            label = parts[k][rows:, :rows].astype(jnp.float32)[:1]
            labels[k] = label, jnp.min(label), jnp.max(label)
        return labels[k]

    def tile(r, c):
        sims = lax.dot_general(
            parts[n_right + c][:rows],
            parts[r][:rows],
            (((1,), (1,)), ((), ())),
            preferred_element_type=jnp.float32,
        )
        for b in range(blocks):
            at = slice(b * BLOCK, (b + 1) * BLOCK)
            label = jnp.broadcast_to(labels[n_right + c][0][:, at], (BLOCK, BLOCK)).T
            label = jnp.concatenate([label] * blocks, axis=1)
            same = label == labels[r][0]
            part = sims[at]
            if own_first and c == 0 and r == 0:
                index = lax.broadcasted_iota(jnp.int32, part.shape, 0) + b * BLOCK
                same &= index != lax.broadcasted_iota(jnp.int32, part.shape, 1)
            part = jnp.where(same, part, -1.0)
            row = places[c] + b
            outs[r][row : row + 1, :] = jnp.max(part, axis=0, keepdims=True)

    todo = [
        (r, c)
        for c in range(len(places))
        for r in range(n_right)
        if r >= n_before or places[c] >= before[r].shape[0]
    ]
    for r, c in sorted(todo, key=lambda rc: (len(copies[n_right + rc[1]]), len(copies[rc[0]]))):
        right, left = labels_of(r), labels_of(n_right + c)
        pl.when((left[1] <= right[2]) & (right[1] <= left[2]))(functools.partial(tile, r, c))


def tiles(name, rights, lefts, places, own_first, before=(), token=None, flops=None):
    parts = list(rights) + list(lefts)
    counts = tuple(len(part) if isinstance(part, list) else 0 for part in parts)
    operands = [piece for part in parts for piece in (part if isinstance(part, list) else [part])]
    height_in, depth = operands[0].shape
    rows = height_in - LABEL_ROWS
    height = -(-(places[-1] + rows // BLOCK) // 8) * 8
    if flops is None:
        flops = 2 * len(rights) * len(lefts) * rows * rows * depth
    vmem, anywhere = pl.BlockSpec(memory_space=pltpu.VMEM), pl.BlockSpec(memory_space=pl.ANY)
    specs = [spec for count in counts for spec in ([anywhere] * count if count else [vmem])]
    extra = list(before) + ([] if token is None else [token])
    scratch = [pltpu.VMEM((height_in, depth), jnp.bfloat16) for count in counts if count]
    if scratch:
        scratch.append(pltpu.SemaphoreType.DMA((sum(counts),)))
    return pl.pallas_call(
        functools.partial(tile_kernel, counts, len(rights), tuple(places), rows, own_first, len(before), len(extra) - len(before)),
        name=name,
        in_specs=specs + [vmem] * len(extra),
        out_specs=[vmem] * len(rights),
        out_shape=[jax.ShapeDtypeStruct((height, rows), jnp.float32)] * len(rights),
        scratch_shapes=scratch,
        compiler_params=pltpu.CompilerParams(vmem_limit_bytes=VMEM_TILES),
        cost_estimate=pl.CostEstimate(
            flops=flops, bytes_accessed=2 * len(operands) * rows * depth, transcendentals=0
        ),
    )(*operands, *extra)


def local(embeddings, cluster_id, requests, pair_left, pair_right):
    n = lax.axis_size(AXIS)
    rows = embeddings.shape[0]
    blk_dev = rows // BLOCK

    def swap(x, bit):
        return lax.ppermute(x, AXIS, [(i, i ^ bit) for i in range(n)])

    def from_above(x):
        return lax.ppermute(x, AXIS, [(i + PLANE, i) for i in range(n - PLANE)])

    def from_below(x):
        return lax.ppermute(x, AXIS, [(i, i + PLANE) for i in range(n - PLANE)])

    def owners_best(parts, cap):
        mine, for_x, for_y, for_across = parts
        returned = jnp.stack([mine, swap(for_x, 2), swap(for_y, 4), swap(for_across, 6)])
        return jnp.maximum(jnp.max(jnp.minimum(returned, cap), axis=(0, 1)), -1.0)

    unit = normalise(embeddings, cluster_id)
    along_x, along_y = swap(unit, 2), swap(unit, 4)
    above, below = from_above(unit), from_below(unit)
    twin = swap(unit, 1)
    message = message_of(requests, pair_left, pair_right, cluster_id)
    along_x, message = lax.optimization_barrier((along_x, message))
    first, second = halves(along_x, along_y)
    pieces = [swap(first, 4), swap(second, 2)]
    along_x, first = lax.optimization_barrier((along_x, first))
    above_twin, below_twin = swap(above, 1), swap(below, 1)

    heard = lax.all_to_all(message, AXIS, split_axis=0, concat_axis=0, tiled=True)

    plane_places = [0, blk_dev]
    next_places = [8 + blk_dev * k for k in range(4)]
    lefts = [[above], above_twin, [below], below_twin]
    near_rights = [unit, along_x, along_y]
    plane_parts = tiles("plane_tiles", near_rights, [unit, twin], plane_places, True)
    token = arrived(pieces)
    parts = tiles(
        "all_tiles",
        near_rights + [pieces],
        [unit, twin] + lefts,
        plane_places + next_places,
        False,
        plane_parts,
        token,
        flops=0,
    )
    cap, span = cover(heard, 1, blk_dev, rows)
    best = owners_best(parts, cap)

    def further(best):
        def body(carry):
            offset, best, above, below = carry
            above, below = from_above(above), from_below(below)
            lefts = [above, swap(above, 1), below, swap(below, 1)]
            parts = tiles(
                "further_tiles",
                near_rights + [pieces],
                lefts,
                [blk_dev * k for k in range(4)],
                False,
            )
            cap, _ = cover(heard, offset, blk_dev, rows)
            best = jnp.maximum(best, owners_best(parts, cap[:, 8:]))
            return offset + 1, best, above, below

        return lax.while_loop(lambda carry: carry[0] <= span, body, (jnp.int32(2), best, above, below))[1]

    return lax.cond(span >= 2, further, lambda best: best, best)


def solution(mesh):
    in_specs = (P(AXIS, None), P(AXIS), P(AXIS), P(AXIS), P(AXIS))
    return jax.shard_map(local, mesh=mesh, in_specs=in_specs, out_specs=P(AXIS), check_vma=False)
```

```python
import functools

import jax
import jax.numpy as jnp
from jax import lax
from jax.experimental import pallas as pl
from jax.experimental.pallas import tpu as pltpu
from jax.sharding import PartitionSpec as P

BLOCK = 128
CLUSTERS = 16
PLANE = 8
JOIN_COST = 10_000_000_000
AXIS = "dev"
LABEL_ROWS = 16
VMEM_TILES = 8 * 1024 * 1024


def normalise_kernel(x_hbm, cluster_hbm, unit_ref, x_ref, cluster_ref, sems):
    copies = [
        pltpu.make_async_copy(x_hbm, x_ref, sems.at[0]),
        pltpu.make_async_copy(cluster_hbm, cluster_ref, sems.at[1]),
    ]
    for copy in copies:
        copy.start()
    rows, depth = x_ref.shape
    unit_ref[rows:] = jnp.zeros((LABEL_ROWS, depth), jnp.bfloat16)
    copies[1].wait()
    label = (cluster_ref[...] + 1).astype(jnp.bfloat16)
    unit_ref[rows:, :rows] = jnp.broadcast_to(label, (LABEL_ROWS, rows))
    copies[0].wait()
    values = x_ref[...].astype(jnp.float32)
    norm = lax.rsqrt(jnp.sum(values * values, axis=-1, keepdims=True) + 1e-06)
    unit_ref[:rows] = (values * norm).astype(jnp.bfloat16)


def normalise(x, cluster_id):
    rows, depth = x.shape
    return pl.pallas_call(
        normalise_kernel,
        name="normalise",
        in_specs=[pl.BlockSpec(memory_space=pltpu.HBM)] * 2,
        out_shape=jax.ShapeDtypeStruct((rows + LABEL_ROWS, depth), jnp.bfloat16),
        scratch_shapes=[
            pltpu.VMEM((rows, depth), x.dtype),
            pltpu.VMEM((1, rows), jnp.int32),
            pltpu.SemaphoreType.DMA((2,)),
        ],
        compiler_params=pltpu.CompilerParams(vmem_limit_bytes=60 * 1024 * 1024),
    )(x, cluster_id.reshape(1, rows))


def message_kernel(n, left_ref, right_ref, request_ref, cluster_ref, out_ref):
    def dot(a, b):
        return lax.dot_general(a, b, (((1,), (1,)), ((), ())), preferred_element_type=jnp.float32)

    def hot(count, ref):
        index = lax.broadcasted_iota(jnp.int32, (count, ref.shape[1]), 0)
        return (index == ref[...]).astype(jnp.float32).astype(jnp.bfloat16)

    left, right, cluster = hot(n, left_ref), hot(n, right_ref), hot(CLUSTERS, cluster_ref)
    out_ref[...] = jnp.zeros(out_ref.shape, jnp.float32)
    out_ref[:, 0, :n] = dot(left, right) + dot(right, left)
    out_ref[:, 0, n : 2 * n] = jnp.broadcast_to(request_ref[...].astype(jnp.float32), (n, n))
    counts = dot(jnp.ones((n, cluster.shape[1]), jnp.bfloat16), cluster)
    out_ref[:, 0, 2 * n : 2 * n + CLUSTERS] = counts


def message_of(requests, pair_left, pair_right, cluster_id):
    n = requests.shape[0]
    width = -(-(2 * n + CLUSTERS) // BLOCK) * BLOCK
    return pl.pallas_call(
        functools.partial(message_kernel, n),
        name="message",
        out_shape=jax.ShapeDtypeStruct((n, 1, width), jnp.float32),
        compiler_params=pltpu.CompilerParams(vmem_limit_bytes=4 * 1024 * 1024),
    )(pair_left.reshape(1, -1), pair_right.reshape(1, -1), requests.reshape(1, -1), cluster_id.reshape(1, -1))


def cover_kernel(blk_dev, rows, offset_ref, heard_ref, cap_ref, span_ref):
    n = heard_ref.shape[0]
    me = lax.axis_index(AXIS)

    def iota(shape, dimension):
        return lax.broadcasted_iota(jnp.int32, shape, dimension)

    def hot(mask):
        return mask.astype(jnp.float32)

    listed = heard_ref[:, 0, :n] > 0
    requests = heard_ref[:, 0, n : 2 * n]
    own = jnp.sum(jnp.where(iota((n, n), 1) == me, requests, 0.0), axis=1, keepdims=True)
    owns = hot(own == (iota((n, rows), 1) // BLOCK).astype(jnp.float32)).astype(jnp.bfloat16)
    height = cap_ref.shape[1]
    at = iota((4 * height, n), 0)
    source, at = at // height, at % height
    near = at < 8
    at = jnp.where(near, at, at - 8)
    part, block = at // blk_dev, at % blk_dev
    step = jnp.where(near, 0, jnp.where(part < 2, offset_ref[0], -offset_ref[0]))
    device = ((2 * source + part % 2) ^ me) + step * PLANE
    device = jnp.where(near & (part >= 2), -1, device)
    total = jnp.zeros((4 * height, rows), jnp.float32)
    for b in range(blk_dev):
        asked = hot(listed & (requests == b)).T.astype(jnp.bfloat16)
        count = jnp.dot(asked, owns, preferred_element_type=jnp.float32)
        pick = hot((iota((4 * height, n), 1) == device) & (block == b)).astype(jnp.bfloat16)
        total += jnp.dot(pick, hot(count > 0).astype(jnp.bfloat16), preferred_element_type=jnp.float32)
    cap_ref[...] = jnp.where(total > 0, jnp.inf, -1.0).reshape(cap_ref.shape)
    present = heard_ref[:, 0, 2 * n : 2 * n + CLUSTERS] > 0
    plane = (iota((n, CLUSTERS), 0) // PLANE).astype(jnp.float32)
    first = jnp.min(jnp.where(present, plane, float(n)), axis=0, keepdims=True)
    last = jnp.max(jnp.where(present, plane, -1.0), axis=0, keepdims=True)
    span_ref[0] = jnp.max(last - first).astype(jnp.int32)


def cover(heard, offset, blk_dev, rows):
    cap, span = pl.pallas_call(
        functools.partial(cover_kernel, blk_dev, rows),
        name="cover",
        in_specs=[pl.BlockSpec(memory_space=pltpu.SMEM), pl.BlockSpec(memory_space=pltpu.VMEM)],
        out_specs=[pl.BlockSpec(memory_space=pltpu.VMEM), pl.BlockSpec(memory_space=pltpu.SMEM)],
        out_shape=[
            jax.ShapeDtypeStruct((4, 8 + 4 * blk_dev, rows), jnp.float32),
            jax.ShapeDtypeStruct((1,), jnp.int32),
        ],
        compiler_params=pltpu.CompilerParams(vmem_limit_bytes=8 * 1024 * 1024),
    )(jnp.asarray(offset, jnp.int32).reshape(1), heard)
    return cap, span[0]


def half_kernel(top, x_ref, half_ref):
    half_ref[...] = x_ref[top : top + half_ref.shape[0]]


def half_of(x, lower):
    half = (x.shape[0] - LABEL_ROWS) // 2
    return pl.pallas_call(
        functools.partial(half_kernel, half if lower else 0),
        name="lower_half" if lower else "upper_half",
        out_shape=jax.ShapeDtypeStruct((half + LABEL_ROWS * lower, x.shape[1]), x.dtype),
        compiler_params=pltpu.CompilerParams(vmem_limit_bytes=4 * 1024 * 1024),
        cost_estimate=pl.CostEstimate(flops=0, bytes_accessed=x.size * 2, transcendentals=0),
    )(x)


def arrived_kernel(first_ref, second_ref, token_ref):
    del first_ref, second_ref
    token_ref[...] = jnp.zeros(token_ref.shape, jnp.float32)


def arrived(pieces):
    return pl.pallas_call(
        arrived_kernel,
        name="arrived",
        in_specs=[pl.BlockSpec(memory_space=pl.ANY)] * 2,
        out_shape=jax.ShapeDtypeStruct((8, 128), jnp.float32),
        compiler_params=pltpu.CompilerParams(vmem_limit_bytes=1024 * 1024),
        cost_estimate=pl.CostEstimate(flops=JOIN_COST, bytes_accessed=4096, transcendentals=0),
    )(*pieces)


def tile_kernel(counts, n_right, places, rows, own_first, n_before, n_token, *refs):
    parts, copies = [], []
    n_operands = sum(max(count, 1) for count in counts)
    tail = refs[n_operands + n_before + n_token :]
    outs, down, scratch = tail[:n_right], tail[n_right], tail[n_right + 1 :]
    operands, before = list(refs[:n_operands]), refs[n_operands : n_operands + n_before]
    sem = 0
    for count in counts:
        here, operands = operands[: max(count, 1)], operands[max(count, 1) :]
        if not count:
            parts.append(here[0])
            copies.append([])
            continue
        part, top, own = scratch[sum(1 for c in copies if c)], 0, []
        for piece in here:
            own.append(pltpu.make_async_copy(piece, part.at[pl.ds(top, piece.shape[0])], scratch[-1].at[sem]))
            own[-1].start()
            top, sem = top + piece.shape[0], sem + 1
        parts.append(part)
        copies.append(own)
    for r, out in enumerate(outs):
        out[...] = jnp.full(out.shape, -1.0, jnp.float32)
        if r < n_before:
            out[: before[r].shape[0]] = before[r][...]
    blocks = rows // BLOCK
    labels = {}

    def labels_of(k):
        if k not in labels:
            for copy in copies[k]:
                copy.wait()
            label = parts[k][rows:, :rows].astype(jnp.float32)[:1]
            labels[k] = label, jnp.min(label), jnp.max(label)
            if k >= n_right:
                for b in range(blocks):
                    at = slice(b * BLOCK, (b + 1) * BLOCK)
                    down[k - n_right, at] = jnp.broadcast_to(label[:, at], (BLOCK, BLOCK)).T
        return labels[k]

    def tile(r, c):
        sims = lax.dot_general(
            parts[n_right + c][:rows],
            parts[r][:rows],
            (((1,), (1,)), ((), ())),
            preferred_element_type=jnp.float32,
        )
        for b in range(blocks):
            at = slice(b * BLOCK, (b + 1) * BLOCK)
            label = jnp.concatenate([down[c, at]] * blocks, axis=1)
            same = label == labels[r][0]
            part = sims[at]
            if own_first and c == 0 and r == 0:
                index = lax.broadcasted_iota(jnp.int32, part.shape, 0) + b * BLOCK
                same &= index != lax.broadcasted_iota(jnp.int32, part.shape, 1)
            part = jnp.where(same, part, -1.0)
            row = places[c] + b
            outs[r][row : row + 1, :] = jnp.max(part, axis=0, keepdims=True)

    for chip in range(0, len(places), 2):
        todo = [
            (r, c)
            for c in range(chip, min(chip + 2, len(places)))
            for r in range(n_right)
            if r >= n_before or places[c] >= before[r].shape[0]
        ]
        meet = False
        for r, c in todo:
            right, left = labels_of(r), labels_of(n_right + c)
            meet |= (left[1] <= right[2]) & (right[1] <= left[2])

        def chip_tiles(todo=todo):
            for r, c in todo:
                tile(r, c)

        if own_first:
            chip_tiles()
        else:
            pl.when(meet)(chip_tiles)


def tiles(name, rights, lefts, places, own_first, before=(), token=None, flops=None):
    parts = list(rights) + list(lefts)
    counts = tuple(len(part) if isinstance(part, list) else 0 for part in parts)
    operands = [piece for part in parts for piece in (part if isinstance(part, list) else [part])]
    height_in, depth = operands[0].shape
    rows = height_in - LABEL_ROWS
    height = -(-(places[-1] + rows // BLOCK) // 8) * 8
    if flops is None:
        flops = 2 * len(rights) * len(lefts) * rows * rows * depth
    vmem, anywhere = pl.BlockSpec(memory_space=pltpu.VMEM), pl.BlockSpec(memory_space=pl.ANY)
    specs = [spec for count in counts for spec in ([anywhere] * count if count else [vmem])]
    extra = list(before) + ([] if token is None else [token])
    scratch = [pltpu.VMEM((len(lefts), rows, BLOCK), jnp.float32)]
    scratch += [pltpu.VMEM((height_in, depth), jnp.bfloat16) for count in counts if count]
    if sum(counts):
        scratch.append(pltpu.SemaphoreType.DMA((sum(counts),)))
    return pl.pallas_call(
        functools.partial(tile_kernel, counts, len(rights), tuple(places), rows, own_first, len(before), len(extra) - len(before)),
        name=name,
        in_specs=specs + [vmem] * len(extra),
        out_specs=[vmem] * len(rights),
        out_shape=[jax.ShapeDtypeStruct((height, rows), jnp.float32)] * len(rights),
        scratch_shapes=scratch,
        compiler_params=pltpu.CompilerParams(vmem_limit_bytes=VMEM_TILES),
        cost_estimate=pl.CostEstimate(
            flops=flops, bytes_accessed=2 * len(operands) * rows * depth, transcendentals=0
        ),
    )(*operands, *extra)


def local(embeddings, cluster_id, requests, pair_left, pair_right):
    n = lax.axis_size(AXIS)
    rows = embeddings.shape[0]
    blk_dev = rows // BLOCK

    def swap(x, bit):
        return lax.ppermute(x, AXIS, [(i, i ^ bit) for i in range(n)])

    def from_above(x):
        return lax.ppermute(x, AXIS, [(i + PLANE, i) for i in range(n - PLANE)])

    def from_below(x):
        return lax.ppermute(x, AXIS, [(i, i + PLANE) for i in range(n - PLANE)])

    def owners_best(parts, cap):
        mine, for_x, for_y, for_across = parts
        returned = jnp.stack([mine, swap(for_x, 2), swap(for_y, 4), swap(for_across, 6)])
        return jnp.maximum(jnp.max(jnp.minimum(returned, cap), axis=(0, 1)), -1.0)

    unit = normalise(embeddings, cluster_id)
    along_x, along_y = swap(unit, 2), swap(unit, 4)
    above, below = from_above(unit), from_below(unit)
    twin = swap(unit, 1)
    message = message_of(requests, pair_left, pair_right, cluster_id)
    along_y, _ = lax.optimization_barrier((along_y, message))
    first, second = half_of(along_x, False), half_of(along_y, True)
    pieces = [swap(first, 4), swap(second, 2)]
    along_x, first = lax.optimization_barrier((along_x, first))
    above_twin, below_twin = swap(above, 1), swap(below, 1)

    heard = lax.all_to_all(message, AXIS, split_axis=0, concat_axis=0, tiled=True)

    plane_places = [0, blk_dev]
    next_places = [8 + blk_dev * k for k in range(4)]
    lefts = [[above], above_twin, [below], below_twin]
    near_rights = [unit, along_x, along_y]
    plane_parts = tiles("plane_tiles", near_rights, [unit, twin], plane_places, True)
    token = arrived(pieces)
    parts = tiles(
        "all_tiles",
        near_rights + [pieces],
        [unit, twin] + lefts,
        plane_places + next_places,
        False,
        plane_parts,
        token,
        flops=0,
    )
    cap, span = cover(heard, 1, blk_dev, rows)
    best = owners_best(parts, cap)

    def further(best):
        def body(carry):
            offset, best, above, below = carry
            above, below = from_above(above), from_below(below)
            lefts = [above, swap(above, 1), below, swap(below, 1)]
            parts = tiles(
                "further_tiles",
                near_rights + [pieces],
                lefts,
                [blk_dev * k for k in range(4)],
                False,
            )
            cap, _ = cover(heard, offset, blk_dev, rows)
            best = jnp.maximum(best, owners_best(parts, cap[:, 8:]))
            return offset + 1, best, above, below

        return lax.while_loop(lambda carry: carry[0] <= span, body, (jnp.int32(2), best, above, below))[1]

    return lax.cond(span >= 2, further, lambda best: best, best)


def solution(mesh):
    in_specs = (P(AXIS, None), P(AXIS), P(AXIS), P(AXIS), P(AXIS))
    return jax.shard_map(local, mesh=mesh, in_specs=in_specs, out_specs=P(AXIS), check_vma=False)
```

```python
import functools

import jax
import jax.numpy as jnp
from jax import lax
from jax.experimental import pallas as pl
from jax.experimental.pallas import tpu as pltpu
from jax.sharding import PartitionSpec as P

BLOCK = 128
CLUSTERS = 16
PLANE = 8
JOIN_COST = 10_000_000_000
AXIS = "dev"
LABEL_ROWS = 16
VMEM_TILES = 8 * 1024 * 1024


def normalise_kernel(x_hbm, cluster_hbm, unit_ref, x_ref, cluster_ref, sems):
    copies = [
        pltpu.make_async_copy(x_hbm, x_ref, sems.at[0]),
        pltpu.make_async_copy(cluster_hbm, cluster_ref, sems.at[1]),
    ]
    for copy in copies:
        copy.start()
    rows, depth = x_ref.shape
    unit_ref[rows:] = jnp.zeros((LABEL_ROWS, depth), jnp.bfloat16)
    copies[1].wait()
    label = (cluster_ref[...] + 1).astype(jnp.bfloat16)
    unit_ref[rows:, :rows] = jnp.broadcast_to(label, (LABEL_ROWS, rows))
    copies[0].wait()
    values = x_ref[...].astype(jnp.float32)
    norm = lax.rsqrt(jnp.sum(values * values, axis=-1, keepdims=True) + 1e-06)
    unit_ref[:rows] = (values * norm).astype(jnp.bfloat16)


def normalise(x, cluster_id):
    rows, depth = x.shape
    return pl.pallas_call(
        normalise_kernel,
        name="normalise",
        in_specs=[pl.BlockSpec(memory_space=pltpu.HBM)] * 2,
        out_shape=jax.ShapeDtypeStruct((rows + LABEL_ROWS, depth), jnp.bfloat16),
        scratch_shapes=[
            pltpu.VMEM((rows, depth), x.dtype),
            pltpu.VMEM((1, rows), jnp.int32),
            pltpu.SemaphoreType.DMA((2,)),
        ],
        compiler_params=pltpu.CompilerParams(vmem_limit_bytes=60 * 1024 * 1024),
    )(x, cluster_id.reshape(1, rows))


def message_kernel(n, left_ref, right_ref, request_ref, cluster_ref, out_ref):
    def dot(a, b):
        return lax.dot_general(a, b, (((1,), (1,)), ((), ())), preferred_element_type=jnp.float32)

    def hot(count, ref):
        index = lax.broadcasted_iota(jnp.int32, (count, ref.shape[1]), 0)
        return (index == ref[...]).astype(jnp.float32).astype(jnp.bfloat16)

    left, right, cluster = hot(n, left_ref), hot(n, right_ref), hot(CLUSTERS, cluster_ref)
    out_ref[...] = jnp.zeros(out_ref.shape, jnp.float32)
    out_ref[:, 0, :n] = dot(left, right) + dot(right, left)
    out_ref[:, 0, n : 2 * n] = jnp.broadcast_to(request_ref[...].astype(jnp.float32), (n, n))
    counts = dot(jnp.ones((n, cluster.shape[1]), jnp.bfloat16), cluster)
    out_ref[:, 0, 2 * n : 2 * n + CLUSTERS] = counts


def message_of(requests, pair_left, pair_right, cluster_id):
    n = requests.shape[0]
    width = -(-(2 * n + CLUSTERS) // BLOCK) * BLOCK
    return pl.pallas_call(
        functools.partial(message_kernel, n),
        name="message",
        out_shape=jax.ShapeDtypeStruct((n, 1, width), jnp.float32),
        compiler_params=pltpu.CompilerParams(vmem_limit_bytes=4 * 1024 * 1024),
    )(pair_left.reshape(1, -1), pair_right.reshape(1, -1), requests.reshape(1, -1), cluster_id.reshape(1, -1))


def cover_kernel(blk_dev, rows, offset_ref, heard_ref, cap_ref, span_ref):
    n = heard_ref.shape[0]
    me = lax.axis_index(AXIS)

    def iota(shape, dimension):
        return lax.broadcasted_iota(jnp.int32, shape, dimension)

    def hot(mask):
        return mask.astype(jnp.float32)

    listed = heard_ref[:, 0, :n] > 0
    requests = heard_ref[:, 0, n : 2 * n]
    own = jnp.sum(jnp.where(iota((n, n), 1) == me, requests, 0.0), axis=1, keepdims=True)
    owns = hot(own == (iota((n, rows), 1) // BLOCK).astype(jnp.float32)).astype(jnp.bfloat16)
    height = cap_ref.shape[1]
    at = iota((4 * height, n), 0)
    source, at = at // height, at % height
    near = at < 8
    at = jnp.where(near, at, at - 8)
    part, block = at // blk_dev, at % blk_dev
    step = jnp.where(near, 0, jnp.where(part < 2, offset_ref[0], -offset_ref[0]))
    device = ((2 * source + part % 2) ^ me) + step * PLANE
    device = jnp.where(near & (part >= 2), -1, device)
    total = jnp.zeros((4 * height, rows), jnp.float32)
    for b in range(blk_dev):
        asked = hot(listed & (requests == b)).T.astype(jnp.bfloat16)
        count = jnp.dot(asked, owns, preferred_element_type=jnp.float32)
        pick = hot((iota((4 * height, n), 1) == device) & (block == b)).astype(jnp.bfloat16)
        total += jnp.dot(pick, hot(count > 0).astype(jnp.bfloat16), preferred_element_type=jnp.float32)
    cap_ref[...] = jnp.where(total > 0, jnp.inf, -1.0).reshape(cap_ref.shape)
    present = heard_ref[:, 0, 2 * n : 2 * n + CLUSTERS] > 0
    plane = (iota((n, CLUSTERS), 0) // PLANE).astype(jnp.float32)
    first = jnp.min(jnp.where(present, plane, float(n)), axis=0, keepdims=True)
    last = jnp.max(jnp.where(present, plane, -1.0), axis=0, keepdims=True)
    span_ref[0] = jnp.max(last - first).astype(jnp.int32)


def cover(heard, offset, blk_dev, rows):
    cap, span = pl.pallas_call(
        functools.partial(cover_kernel, blk_dev, rows),
        name="cover",
        in_specs=[pl.BlockSpec(memory_space=pltpu.SMEM), pl.BlockSpec(memory_space=pltpu.VMEM)],
        out_specs=[pl.BlockSpec(memory_space=pltpu.VMEM), pl.BlockSpec(memory_space=pltpu.SMEM)],
        out_shape=[
            jax.ShapeDtypeStruct((4, 8 + 4 * blk_dev, rows), jnp.float32),
            jax.ShapeDtypeStruct((1,), jnp.int32),
        ],
        compiler_params=pltpu.CompilerParams(vmem_limit_bytes=8 * 1024 * 1024),
    )(jnp.asarray(offset, jnp.int32).reshape(1), heard)
    return cap, span[0]


def half_kernel(top, x_ref, half_ref):
    half_ref[...] = x_ref[top : top + half_ref.shape[0]]


def half_of(x, lower):
    half = (x.shape[0] - LABEL_ROWS) // 2
    return pl.pallas_call(
        functools.partial(half_kernel, half if lower else 0),
        name="lower_half" if lower else "upper_half",
        out_shape=jax.ShapeDtypeStruct((half + LABEL_ROWS * lower, x.shape[1]), x.dtype),
        compiler_params=pltpu.CompilerParams(vmem_limit_bytes=4 * 1024 * 1024),
        cost_estimate=pl.CostEstimate(flops=0, bytes_accessed=x.size * 2, transcendentals=0),
    )(x)


def arrived_kernel(first_ref, second_ref, token_ref):
    del first_ref, second_ref
    token_ref[...] = jnp.zeros(token_ref.shape, jnp.float32)


def arrived(pieces):
    return pl.pallas_call(
        arrived_kernel,
        name="arrived",
        in_specs=[pl.BlockSpec(memory_space=pl.ANY)] * 2,
        out_shape=jax.ShapeDtypeStruct((8, 128), jnp.float32),
        compiler_params=pltpu.CompilerParams(vmem_limit_bytes=1024 * 1024),
        cost_estimate=pl.CostEstimate(flops=JOIN_COST, bytes_accessed=4096, transcendentals=0),
    )(*pieces)


def tile_kernel(counts, n_right, places, rows, own_first, n_before, n_token, keep, *refs):
    parts, copies = [], []
    n_operands = sum(max(count, 1) for count in counts)
    tail = refs[n_operands + n_before + n_token :]
    outs, kept, tail = tail[:n_right], tail[n_right : n_right + len(keep)], tail[n_right + len(keep) :]
    down, scratch = tail[0], tail[1:]
    keeping = {}

    def put_away(k):
        if k in keep:
            at = keep.index(k)
            keeping[k] = pltpu.make_async_copy(parts[k], kept[at], scratch[-1].at[sum(counts) + at])
            keeping[k].start()

    operands, before = list(refs[:n_operands]), refs[n_operands : n_operands + n_before]
    sem = 0
    for count in counts:
        here, operands = operands[: max(count, 1)], operands[max(count, 1) :]
        if not count:
            parts.append(here[0])
            copies.append([])
            put_away(len(parts) - 1)
            continue
        part, top, own = scratch[sum(1 for c in copies if c)], 0, []
        for piece in here:
            own.append(pltpu.make_async_copy(piece, part.at[pl.ds(top, piece.shape[0])], scratch[-1].at[sem]))
            own[-1].start()
            top, sem = top + piece.shape[0], sem + 1
        parts.append(part)
        copies.append(own)
    for r, out in enumerate(outs):
        out[...] = jnp.full(out.shape, -1.0, jnp.float32)
        if r < n_before:
            out[: before[r].shape[0]] = before[r][...]
    blocks = rows // BLOCK
    labels = {}

    def labels_of(k):
        if k not in labels:
            for copy in copies[k]:
                copy.wait()
            if copies[k]:
                put_away(k)
            label = parts[k][rows:, :rows].astype(jnp.float32)[:1]
            labels[k] = label, label[0, 0], label[0, rows - 1]
            if k >= n_right:
                for b in range(blocks):
                    at = slice(b * BLOCK, (b + 1) * BLOCK)
                    down[k - n_right, at] = jnp.broadcast_to(label[:, at], (BLOCK, BLOCK)).T
        return labels[k]

    def tile(r, c):
        sims = lax.dot_general(
            parts[n_right + c][:rows],
            parts[r][:rows],
            (((1,), (1,)), ((), ())),
            preferred_element_type=jnp.float32,
        )
        for b in range(blocks):
            at = slice(b * BLOCK, (b + 1) * BLOCK)
            label = jnp.concatenate([down[c, at]] * blocks, axis=1)
            same = label == labels[r][0]
            part = sims[at]
            if own_first and c == 0 and r == 0:
                index = lax.broadcasted_iota(jnp.int32, part.shape, 0) + b * BLOCK
                same &= index != lax.broadcasted_iota(jnp.int32, part.shape, 1)
            part = jnp.where(same, part, -1.0)
            row = places[c] + b
            outs[r][row : row + 1, :] = jnp.max(part, axis=0, keepdims=True)

    for chip in range(0, len(places), 2):
        todo = [
            (r, c)
            for c in range(chip, min(chip + 2, len(places)))
            for r in range(n_right)
            if r >= n_before or places[c] >= before[r].shape[0]
        ]
        meet = False
        for r, c in todo:
            right, left = labels_of(r), labels_of(n_right + c)
            meet |= (left[1] <= right[2]) & (right[1] <= left[2])

        def chip_tiles(todo=todo):
            for r, c in todo:
                tile(r, c)

        if own_first:
            chip_tiles()
        else:
            pl.when(meet)(chip_tiles)
    for copy in keeping.values():
        copy.wait()


def tiles(name, rights, lefts, places, own_first, before=(), token=None, flops=None, keep=()):
    parts = list(rights) + list(lefts)
    counts = tuple(len(part) if isinstance(part, list) else 0 for part in parts)
    operands = [piece for part in parts for piece in (part if isinstance(part, list) else [part])]
    height_in, depth = operands[0].shape
    rows = height_in - LABEL_ROWS
    height = -(-(places[-1] + rows // BLOCK) // 8) * 8
    if flops is None:
        flops = 2 * len(rights) * len(lefts) * rows * rows * depth
    vmem, anywhere = pl.BlockSpec(memory_space=pltpu.VMEM), pl.BlockSpec(memory_space=pl.ANY)
    specs = [spec for count in counts for spec in ([anywhere] * count if count else [vmem])]
    extra = list(before) + ([] if token is None else [token])
    scratch = [pltpu.VMEM((len(lefts), rows, BLOCK), jnp.float32)]
    scratch += [pltpu.VMEM((height_in, depth), jnp.bfloat16) for count in counts if count]
    if sum(counts) + len(keep):
        scratch.append(pltpu.SemaphoreType.DMA((sum(counts) + len(keep),)))
    return pl.pallas_call(
        functools.partial(tile_kernel, counts, len(rights), tuple(places), rows, own_first, len(before), len(extra) - len(before), keep),
        name=name,
        in_specs=specs + [vmem] * len(extra),
        out_specs=[vmem] * len(rights) + [pl.BlockSpec(memory_space=pltpu.HBM)] * len(keep),
        out_shape=[jax.ShapeDtypeStruct((height, rows), jnp.float32)] * len(rights)
        + [jax.ShapeDtypeStruct((height_in, depth), jnp.bfloat16)] * len(keep),
        scratch_shapes=scratch,
        compiler_params=pltpu.CompilerParams(vmem_limit_bytes=VMEM_TILES),
        cost_estimate=pl.CostEstimate(
            flops=flops, bytes_accessed=2 * len(operands) * rows * depth, transcendentals=0
        ),
    )(*operands, *extra)


def local(embeddings, cluster_id, requests, pair_left, pair_right):
    n = lax.axis_size(AXIS)
    rows = embeddings.shape[0]
    blk_dev = rows // BLOCK

    def swap(x, bit):
        return lax.ppermute(x, AXIS, [(i, i ^ bit) for i in range(n)])

    def from_above(x):
        return lax.ppermute(x, AXIS, [(i + PLANE, i) for i in range(n - PLANE)])

    def from_below(x):
        return lax.ppermute(x, AXIS, [(i, i + PLANE) for i in range(n - PLANE)])

    def owners_best(parts, cap):
        mine, for_x, for_y, for_across = parts
        returned = jnp.stack([mine, swap(for_x, 2), swap(for_y, 4), swap(for_across, 6)])
        return jnp.maximum(jnp.max(jnp.minimum(returned, cap), axis=(0, 1)), -1.0)

    unit = normalise(embeddings, cluster_id)
    along_x, along_y = swap(unit, 2), swap(unit, 4)
    above, below = from_above(unit), from_below(unit)
    twin = swap(unit, 1)
    message = message_of(requests, pair_left, pair_right, cluster_id)
    along_y, _ = lax.optimization_barrier((along_y, message))
    first, second = half_of(along_x, False), half_of(along_y, True)
    pieces = [swap(first, 4), swap(second, 2)]
    along_x, first = lax.optimization_barrier((along_x, first))
    above_twin, below_twin = swap(above, 1), swap(below, 1)

    heard = lax.all_to_all(message, AXIS, split_axis=0, concat_axis=0, tiled=True)

    plane_places = [0, blk_dev]
    next_places = [8 + blk_dev * k for k in range(4)]
    lefts = [[above], above_twin, [below], below_twin]
    near_rights = [unit, along_x, along_y]
    plane_parts = tiles("plane_tiles", near_rights, [unit, twin], plane_places, True)
    token = arrived(pieces)
    *parts, across = tiles(
        "all_tiles",
        near_rights + [pieces],
        [unit, twin] + lefts,
        plane_places + next_places,
        False,
        plane_parts,
        token,
        flops=0,
        keep=(3,),
    )
    cap, span = cover(heard, 1, blk_dev, rows)
    best = owners_best(parts, cap)

    def further(best):
        def body(carry):
            offset, best, above, below = carry
            above, below = from_above(above), from_below(below)
            lefts = [above, swap(above, 1), below, swap(below, 1)]
            parts = tiles(
                "further_tiles",
                near_rights + [across],
                lefts,
                [blk_dev * k for k in range(4)],
                False,
            )
            cap, _ = cover(heard, offset, blk_dev, rows)
            best = jnp.maximum(best, owners_best(parts, cap[:, 8:]))
            return offset + 1, best, above, below

        return lax.while_loop(lambda carry: carry[0] <= span, body, (jnp.int32(2), best, above, below))[1]

    return lax.cond(span >= 2, further, lambda best: best, best)


def solution(mesh):
    in_specs = (P(AXIS, None), P(AXIS), P(AXIS), P(AXIS), P(AXIS))
    return jax.shard_map(local, mesh=mesh, in_specs=in_specs, out_specs=P(AXIS), check_vma=False)
```

```python
import functools

import jax
import jax.numpy as jnp
from jax import lax
from jax.experimental import pallas as pl
from jax.experimental.pallas import tpu as pltpu
from jax.sharding import PartitionSpec as P

BLOCK = 128
CLUSTERS = 16
PLANE = 8
JOIN_COST = 10_000_000_000
AXIS = "dev"
LABEL_ROWS = 16
VMEM_TILES = 8 * 1024 * 1024


def normalise_kernel(x_hbm, cluster_hbm, unit_ref, x_ref, cluster_ref, sems):
    copies = [
        pltpu.make_async_copy(x_hbm, x_ref, sems.at[0]),
        pltpu.make_async_copy(cluster_hbm, cluster_ref, sems.at[1]),
    ]
    for copy in copies:
        copy.start()
    rows, depth = x_ref.shape
    unit_ref[rows:] = jnp.zeros((LABEL_ROWS, depth), jnp.bfloat16)
    copies[1].wait()
    label = (cluster_ref[...] + 1).astype(jnp.bfloat16)
    unit_ref[rows:, :rows] = jnp.broadcast_to(label, (LABEL_ROWS, rows))
    copies[0].wait()
    values = x_ref[...].astype(jnp.float32)
    norm = lax.rsqrt(jnp.sum(values * values, axis=-1, keepdims=True) + 1e-06)
    unit_ref[:rows] = (values * norm).astype(jnp.bfloat16)


def normalise(x, cluster_id):
    rows, depth = x.shape
    return pl.pallas_call(
        normalise_kernel,
        name="normalise",
        in_specs=[pl.BlockSpec(memory_space=pltpu.HBM)] * 2,
        out_shape=jax.ShapeDtypeStruct((rows + LABEL_ROWS, depth), jnp.bfloat16),
        scratch_shapes=[
            pltpu.VMEM((rows, depth), x.dtype),
            pltpu.VMEM((1, rows), jnp.int32),
            pltpu.SemaphoreType.DMA((2,)),
        ],
        compiler_params=pltpu.CompilerParams(vmem_limit_bytes=60 * 1024 * 1024),
    )(x, cluster_id.reshape(1, rows))


def message_kernel(n, left_ref, right_ref, request_ref, cluster_ref, out_ref):
    def dot(a, b):
        return lax.dot_general(a, b, (((1,), (1,)), ((), ())), preferred_element_type=jnp.float32)

    def hot(count, ref):
        index = lax.broadcasted_iota(jnp.int32, (count, ref.shape[1]), 0)
        return (index == ref[...]).astype(jnp.float32).astype(jnp.bfloat16)

    left, right, cluster = hot(n, left_ref), hot(n, right_ref), hot(CLUSTERS, cluster_ref)
    out_ref[...] = jnp.zeros(out_ref.shape, jnp.float32)
    out_ref[:, 0, :n] = dot(left, right) + dot(right, left)
    out_ref[:, 0, n : 2 * n] = jnp.broadcast_to(request_ref[...].astype(jnp.float32), (n, n))
    counts = dot(jnp.ones((n, cluster.shape[1]), jnp.bfloat16), cluster)
    out_ref[:, 0, 2 * n : 2 * n + CLUSTERS] = counts


def message_of(requests, pair_left, pair_right, cluster_id):
    n = requests.shape[0]
    width = -(-(2 * n + CLUSTERS) // BLOCK) * BLOCK
    return pl.pallas_call(
        functools.partial(message_kernel, n),
        name="message",
        out_shape=jax.ShapeDtypeStruct((n, 1, width), jnp.float32),
        compiler_params=pltpu.CompilerParams(vmem_limit_bytes=4 * 1024 * 1024),
    )(pair_left.reshape(1, -1), pair_right.reshape(1, -1), requests.reshape(1, -1), cluster_id.reshape(1, -1))


def cover_kernel(blk_dev, rows, offset_ref, heard_ref, cap_ref, span_ref):
    n = heard_ref.shape[0]
    me = lax.axis_index(AXIS)

    def iota(shape, dimension):
        return lax.broadcasted_iota(jnp.int32, shape, dimension)

    def hot(mask):
        return mask.astype(jnp.float32)

    listed = heard_ref[:, 0, :n] > 0
    requests = heard_ref[:, 0, n : 2 * n]
    own = jnp.sum(jnp.where(iota((n, n), 1) == me, requests, 0.0), axis=1, keepdims=True)
    owns = hot(own == (iota((n, rows), 1) // BLOCK).astype(jnp.float32)).astype(jnp.bfloat16)
    height = cap_ref.shape[1]
    at = iota((4 * height, n), 0)
    source, at = at // height, at % height
    near = at < 8
    at = jnp.where(near, at, at - 8)
    part, block = at // blk_dev, at % blk_dev
    step = jnp.where(near, 0, jnp.where(part < 2, offset_ref[0], -offset_ref[0]))
    device = ((2 * source + part % 2) ^ me) + step * PLANE
    device = jnp.where(near & (part >= 2), -1, device)
    total = jnp.zeros((4 * height, rows), jnp.float32)
    for b in range(blk_dev):
        asked = hot(listed & (requests == b)).T.astype(jnp.bfloat16)
        count = jnp.dot(asked, owns, preferred_element_type=jnp.float32)
        pick = hot((iota((4 * height, n), 1) == device) & (block == b)).astype(jnp.bfloat16)
        total += jnp.dot(pick, hot(count > 0).astype(jnp.bfloat16), preferred_element_type=jnp.float32)
    cap_ref[...] = jnp.where(total > 0, jnp.inf, -1.0).reshape(cap_ref.shape)
    present = heard_ref[:, 0, 2 * n : 2 * n + CLUSTERS] > 0
    plane = (iota((n, CLUSTERS), 0) // PLANE).astype(jnp.float32)
    first = jnp.min(jnp.where(present, plane, float(n)), axis=0, keepdims=True)
    last = jnp.max(jnp.where(present, plane, -1.0), axis=0, keepdims=True)
    span_ref[0] = jnp.max(last - first).astype(jnp.int32)


def cover(heard, offset, blk_dev, rows):
    cap, span = pl.pallas_call(
        functools.partial(cover_kernel, blk_dev, rows),
        name="cover",
        in_specs=[pl.BlockSpec(memory_space=pltpu.SMEM), pl.BlockSpec(memory_space=pltpu.VMEM)],
        out_specs=[pl.BlockSpec(memory_space=pltpu.VMEM), pl.BlockSpec(memory_space=pltpu.SMEM)],
        out_shape=[
            jax.ShapeDtypeStruct((4, 8 + 4 * blk_dev, rows), jnp.float32),
            jax.ShapeDtypeStruct((1,), jnp.int32),
        ],
        compiler_params=pltpu.CompilerParams(vmem_limit_bytes=8 * 1024 * 1024),
    )(jnp.asarray(offset, jnp.int32).reshape(1), heard)
    return cap, span[0]


def half_kernel(top, x_ref, half_ref):
    half_ref[...] = x_ref[top : top + half_ref.shape[0]]


def half_of(x, lower):
    half = (x.shape[0] - LABEL_ROWS) // 2
    return pl.pallas_call(
        functools.partial(half_kernel, half if lower else 0),
        name="lower_half" if lower else "upper_half",
        out_shape=jax.ShapeDtypeStruct((half + LABEL_ROWS * lower, x.shape[1]), x.dtype),
        compiler_params=pltpu.CompilerParams(vmem_limit_bytes=4 * 1024 * 1024),
        cost_estimate=pl.CostEstimate(flops=0, bytes_accessed=x.size * 2, transcendentals=0),
    )(x)


def arrived_kernel(first_ref, second_ref, token_ref):
    del first_ref, second_ref
    token_ref[...] = jnp.zeros(token_ref.shape, jnp.float32)


def arrived(pieces):
    return pl.pallas_call(
        arrived_kernel,
        name="arrived",
        in_specs=[pl.BlockSpec(memory_space=pl.ANY)] * 2,
        out_shape=jax.ShapeDtypeStruct((8, 128), jnp.float32),
        compiler_params=pltpu.CompilerParams(vmem_limit_bytes=1024 * 1024),
        cost_estimate=pl.CostEstimate(flops=JOIN_COST, bytes_accessed=4096, transcendentals=0),
    )(*pieces)


def tile_kernel(counts, n_right, places, groups, rows, own_first, n_before, done, n_token, keep, *refs):
    parts, copies = [], []
    n_operands = sum(max(count, 1) for count in counts)
    tail = refs[n_operands + n_before + n_token :]
    outs, kept, tail = tail[:n_right], tail[n_right : n_right + len(keep)], tail[n_right + len(keep) :]
    down, scratch = tail[0], tail[1:]
    keeping = {}

    def put_away(k):
        if k in keep:
            at = keep.index(k)
            keeping[k] = pltpu.make_async_copy(parts[k], kept[at], scratch[-1].at[sum(counts) + at])
            keeping[k].start()

    operands, before = list(refs[:n_operands]), refs[n_operands : n_operands + n_before]
    sem = 0
    for count in counts:
        here, operands = operands[: max(count, 1)], operands[max(count, 1) :]
        if not count:
            parts.append(here[0])
            copies.append([])
            put_away(len(parts) - 1)
            continue
        part, top, own = scratch[sum(1 for c in copies if c)], 0, []
        for piece in here:
            own.append(pltpu.make_async_copy(piece, part.at[pl.ds(top, piece.shape[0])], scratch[-1].at[sem]))
            own[-1].start()
            top, sem = top + piece.shape[0], sem + 1
        parts.append(part)
        copies.append(own)
    for r, out in enumerate(outs):
        out[...] = jnp.full(out.shape, -1.0, jnp.float32)
        if r < n_before:
            out[: before[r].shape[0]] = before[r][...]
    blocks = rows // BLOCK
    labels = {}

    def labels_of(k):
        if k not in labels:
            for copy in copies[k]:
                copy.wait()
            if copies[k]:
                put_away(k)
            label = parts[k][rows:, :rows].astype(jnp.float32)[:1]
            labels[k] = label, label[0, 0], label[0, rows - 1]
            if k >= n_right:
                for b in range(blocks):
                    at = slice(b * BLOCK, (b + 1) * BLOCK)
                    down[k - n_right, at] = jnp.broadcast_to(label[:, at], (BLOCK, BLOCK)).T
        return labels[k]

    def tile(r, c):
        sims = lax.dot_general(
            parts[n_right + c][:rows],
            parts[r][:rows],
            (((1,), (1,)), ((), ())),
            preferred_element_type=jnp.float32,
        )
        for b in range(blocks):
            at = slice(b * BLOCK, (b + 1) * BLOCK)
            label = jnp.concatenate([down[c, at]] * blocks, axis=1)
            same = label == labels[r][0]
            part = sims[at]
            if own_first and c == 0 and r == 0:
                index = lax.broadcasted_iota(jnp.int32, part.shape, 0) + b * BLOCK
                same &= index != lax.broadcasted_iota(jnp.int32, part.shape, 1)
            part = jnp.where(same, part, -1.0)
            row = places[c] + b
            outs[r][row : row + 1, :] = jnp.max(part, axis=0, keepdims=True)

    for group in groups:
        todo = [(r, c) for c in group for r in range(n_right) if r >= n_before or c not in done]
        meet = False
        for r, c in todo:
            right, left = labels_of(r), labels_of(n_right + c)
            meet |= (left[1] <= right[2]) & (right[1] <= left[2])

        def group_tiles(todo=todo):
            for r, c in todo:
                tile(r, c)

        if own_first and 0 in group:
            group_tiles()
        else:
            pl.when(meet)(group_tiles)
    for copy in keeping.values():
        copy.wait()


def tiles(name, rights, lefts, places, groups, own_first, before=(), done=(), token=None, flops=None, keep=()):
    parts = list(rights) + list(lefts)
    counts = tuple(len(part) if isinstance(part, list) else 0 for part in parts)
    operands = [piece for part in parts for piece in (part if isinstance(part, list) else [part])]
    height_in, depth = operands[0].shape
    rows = height_in - LABEL_ROWS
    height = -(-(places[-1] + rows // BLOCK) // 8) * 8
    if flops is None:
        flops = 2 * len(rights) * len(lefts) * rows * rows * depth
    vmem, anywhere = pl.BlockSpec(memory_space=pltpu.VMEM), pl.BlockSpec(memory_space=pl.ANY)
    specs = [spec for count in counts for spec in ([anywhere] * count if count else [vmem])]
    extra = list(before) + ([] if token is None else [token])
    scratch = [pltpu.VMEM((len(lefts), rows, BLOCK), jnp.float32)]
    scratch += [pltpu.VMEM((height_in, depth), jnp.bfloat16) for count in counts if count]
    if sum(counts) + len(keep):
        scratch.append(pltpu.SemaphoreType.DMA((sum(counts) + len(keep),)))
    return pl.pallas_call(
        functools.partial(tile_kernel, counts, len(rights), tuple(places), groups, rows, own_first, len(before), done, len(extra) - len(before), keep),
        name=name,
        in_specs=specs + [vmem] * len(extra),
        out_specs=[vmem] * len(rights) + [pl.BlockSpec(memory_space=pltpu.HBM)] * len(keep),
        out_shape=[jax.ShapeDtypeStruct((height, rows), jnp.float32)] * len(rights)
        + [jax.ShapeDtypeStruct((height_in, depth), jnp.bfloat16)] * len(keep),
        scratch_shapes=scratch,
        compiler_params=pltpu.CompilerParams(vmem_limit_bytes=VMEM_TILES),
        cost_estimate=pl.CostEstimate(
            flops=flops, bytes_accessed=2 * len(operands) * rows * depth, transcendentals=0
        ),
    )(*operands, *extra)


def local(embeddings, cluster_id, requests, pair_left, pair_right):
    n = lax.axis_size(AXIS)
    rows = embeddings.shape[0]
    blk_dev = rows // BLOCK

    def swap(x, bit):
        return lax.ppermute(x, AXIS, [(i, i ^ bit) for i in range(n)])

    def from_above(x):
        return lax.ppermute(x, AXIS, [(i + PLANE, i) for i in range(n - PLANE)])

    def from_below(x):
        return lax.ppermute(x, AXIS, [(i, i + PLANE) for i in range(n - PLANE)])

    def owners_best(parts, cap):
        mine, for_x, for_y, for_across = parts
        returned = jnp.stack([mine, swap(for_x, 2), swap(for_y, 4), swap(for_across, 6)])
        return jnp.maximum(jnp.max(jnp.minimum(returned, cap), axis=(0, 1)), -1.0)

    unit = normalise(embeddings, cluster_id)
    along_x, along_y = swap(unit, 2), swap(unit, 4)
    above, below = from_above(unit), from_below(unit)
    twin = swap(unit, 1)
    message = message_of(requests, pair_left, pair_right, cluster_id)
    along_y, _ = lax.optimization_barrier((along_y, message))
    first, second = half_of(along_x, False), half_of(along_y, True)
    pieces = [swap(first, 4), swap(second, 2)]
    along_x, first = lax.optimization_barrier((along_x, first))
    above_twin, below_twin = swap(above, 1), swap(below, 1)

    heard = lax.all_to_all(message, AXIS, split_axis=0, concat_axis=0, tiled=True)

    places = [0, blk_dev] + [8 + blk_dev * k for k in range(4)]
    near_rights = [unit, along_x, along_y]
    known = tiles(
        "plane_tiles",
        near_rights,
        [unit, twin, [above], [below]],
        [places[k] for k in (0, 1, 2, 4)],
        ((0, 1), (2,), (3,)),
        True,
    )
    token = arrived(pieces)
    *parts, across = tiles(
        "all_tiles",
        near_rights + [pieces],
        [unit, twin, [above], above_twin, [below], below_twin],
        places,
        ((0, 1), (2, 3), (4, 5)),
        False,
        known,
        (0, 1, 2, 4),
        token,
        flops=0,
        keep=(3,),
    )
    cap, span = cover(heard, 1, blk_dev, rows)
    best = owners_best(parts, cap)

    def further(best):
        def body(carry):
            offset, best, above, below = carry
            above, below = from_above(above), from_below(below)
            lefts = [above, swap(above, 1), below, swap(below, 1)]
            parts = tiles(
                "further_tiles",
                near_rights + [across],
                lefts,
                [blk_dev * k for k in range(4)],
                ((0, 1), (2, 3)),
                False,
            )
            cap, _ = cover(heard, offset, blk_dev, rows)
            best = jnp.maximum(best, owners_best(parts, cap[:, 8:]))
            return offset + 1, best, above, below

        return lax.while_loop(lambda carry: carry[0] <= span, body, (jnp.int32(2), best, above, below))[1]

    return lax.cond(span >= 2, further, lambda best: best, best)


def solution(mesh):
    in_specs = (P(AXIS, None), P(AXIS), P(AXIS), P(AXIS), P(AXIS))
    return jax.shard_map(local, mesh=mesh, in_specs=in_specs, out_specs=P(AXIS), check_vma=False)
```

```python
import functools

import jax
import jax.numpy as jnp
from jax import lax
from jax.experimental import pallas as pl
from jax.experimental.pallas import tpu as pltpu
from jax.sharding import PartitionSpec as P

BLOCK = 128
CLUSTERS = 16
PLANE = 8
JOIN_COST = 10_000_000_000
AXIS = "dev"
LABEL_ROWS = 16
VMEM_TILES = 8 * 1024 * 1024


def normalise_kernel(x_hbm, cluster_hbm, unit_ref, x_ref, cluster_ref, sems):
    copies = [
        pltpu.make_async_copy(x_hbm, x_ref, sems.at[0]),
        pltpu.make_async_copy(cluster_hbm, cluster_ref, sems.at[1]),
    ]
    for copy in copies:
        copy.start()
    rows, depth = x_ref.shape
    unit_ref[rows:] = jnp.zeros((LABEL_ROWS, depth), jnp.bfloat16)
    copies[1].wait()
    label = (cluster_ref[...] + 1).astype(jnp.bfloat16)
    unit_ref[rows:, :rows] = jnp.broadcast_to(label, (LABEL_ROWS, rows))
    copies[0].wait()
    values = x_ref[...].astype(jnp.float32)
    norm = lax.rsqrt(jnp.sum(values * values, axis=-1, keepdims=True) + 1e-06)
    unit_ref[:rows] = (values * norm).astype(jnp.bfloat16)


def normalise(x, cluster_id):
    rows, depth = x.shape
    return pl.pallas_call(
        normalise_kernel,
        name="normalise",
        in_specs=[pl.BlockSpec(memory_space=pltpu.HBM)] * 2,
        out_shape=jax.ShapeDtypeStruct((rows + LABEL_ROWS, depth), jnp.bfloat16),
        scratch_shapes=[
            pltpu.VMEM((rows, depth), x.dtype),
            pltpu.VMEM((1, rows), jnp.int32),
            pltpu.SemaphoreType.DMA((2,)),
        ],
        compiler_params=pltpu.CompilerParams(vmem_limit_bytes=60 * 1024 * 1024),
    )(x, cluster_id.reshape(1, rows))


def message_kernel(n, left_ref, right_ref, request_ref, cluster_ref, out_ref):
    def dot(a, b):
        return lax.dot_general(a, b, (((1,), (1,)), ((), ())), preferred_element_type=jnp.float32)

    def hot(count, ref):
        index = lax.broadcasted_iota(jnp.int32, (count, ref.shape[1]), 0)
        return (index == ref[...]).astype(jnp.float32).astype(jnp.bfloat16)

    left, right, cluster = hot(n, left_ref), hot(n, right_ref), hot(CLUSTERS, cluster_ref)
    out_ref[...] = jnp.zeros(out_ref.shape, jnp.float32)
    out_ref[:, 0, :n] = dot(left, right) + dot(right, left)
    out_ref[:, 0, n : 2 * n] = jnp.broadcast_to(request_ref[...].astype(jnp.float32), (n, n))
    counts = dot(jnp.ones((n, cluster.shape[1]), jnp.bfloat16), cluster)
    out_ref[:, 0, 2 * n : 2 * n + CLUSTERS] = counts


def message_of(requests, pair_left, pair_right, cluster_id):
    n = requests.shape[0]
    width = -(-(2 * n + CLUSTERS) // BLOCK) * BLOCK
    return pl.pallas_call(
        functools.partial(message_kernel, n),
        name="message",
        out_shape=jax.ShapeDtypeStruct((n, 1, width), jnp.float32),
        compiler_params=pltpu.CompilerParams(vmem_limit_bytes=4 * 1024 * 1024),
    )(pair_left.reshape(1, -1), pair_right.reshape(1, -1), requests.reshape(1, -1), cluster_id.reshape(1, -1))


def cover_kernel(blk_dev, rows, offset_ref, heard_ref, cap_ref, span_ref):
    n = heard_ref.shape[0]
    me = lax.axis_index(AXIS)

    def iota(shape, dimension):
        return lax.broadcasted_iota(jnp.int32, shape, dimension)

    def hot(mask):
        return mask.astype(jnp.float32)

    listed = heard_ref[:, 0, :n] > 0
    requests = heard_ref[:, 0, n : 2 * n]
    own = jnp.sum(jnp.where(iota((n, n), 1) == me, requests, 0.0), axis=1, keepdims=True)
    owns = hot(own == (iota((n, rows), 1) // BLOCK).astype(jnp.float32)).astype(jnp.bfloat16)
    height = cap_ref.shape[1]
    at = iota((4 * height, n), 0)
    source, at = at // height, at % height
    near = at < 8
    at = jnp.where(near, at, at - 8)
    part, block = at // blk_dev, at % blk_dev
    step = jnp.where(near, 0, jnp.where(part < 2, offset_ref[0], -offset_ref[0]))
    device = ((2 * source + part % 2) ^ me) + step * PLANE
    device = jnp.where(near & (part >= 2), -1, device)
    total = jnp.zeros((4 * height, rows), jnp.float32)
    for b in range(blk_dev):
        asked = hot(listed & (requests == b)).T.astype(jnp.bfloat16)
        count = jnp.dot(asked, owns, preferred_element_type=jnp.float32)
        pick = hot((iota((4 * height, n), 1) == device) & (block == b)).astype(jnp.bfloat16)
        total += jnp.dot(pick, hot(count > 0).astype(jnp.bfloat16), preferred_element_type=jnp.float32)
    cap_ref[...] = jnp.where(total > 0, jnp.inf, -1.0).reshape(cap_ref.shape)
    present = heard_ref[:, 0, 2 * n : 2 * n + CLUSTERS] > 0
    plane = (iota((n, CLUSTERS), 0) // PLANE).astype(jnp.float32)
    first = jnp.min(jnp.where(present, plane, float(n)), axis=0, keepdims=True)
    last = jnp.max(jnp.where(present, plane, -1.0), axis=0, keepdims=True)
    span_ref[0] = jnp.max(last - first).astype(jnp.int32)


def cover(heard, offset, blk_dev, rows):
    cap, span = pl.pallas_call(
        functools.partial(cover_kernel, blk_dev, rows),
        name="cover",
        in_specs=[pl.BlockSpec(memory_space=pltpu.SMEM), pl.BlockSpec(memory_space=pltpu.VMEM)],
        out_specs=[pl.BlockSpec(memory_space=pltpu.VMEM), pl.BlockSpec(memory_space=pltpu.SMEM)],
        out_shape=[
            jax.ShapeDtypeStruct((4, 8 + 4 * blk_dev, rows), jnp.float32),
            jax.ShapeDtypeStruct((1,), jnp.int32),
        ],
        compiler_params=pltpu.CompilerParams(vmem_limit_bytes=8 * 1024 * 1024),
    )(jnp.asarray(offset, jnp.int32).reshape(1), heard)
    return cap, span[0]


def half_kernel(top, x_ref, half_ref):
    half_ref[...] = x_ref[top : top + half_ref.shape[0]]


def half_of(x, lower):
    half = (x.shape[0] - LABEL_ROWS) // 2
    return pl.pallas_call(
        functools.partial(half_kernel, half if lower else 0),
        name="lower_half" if lower else "upper_half",
        out_shape=jax.ShapeDtypeStruct((half + LABEL_ROWS * lower, x.shape[1]), x.dtype),
        compiler_params=pltpu.CompilerParams(vmem_limit_bytes=4 * 1024 * 1024),
        cost_estimate=pl.CostEstimate(flops=0, bytes_accessed=x.size * 2, transcendentals=0),
    )(x)


def arrived_kernel(first_ref, second_ref, token_ref):
    del first_ref, second_ref
    token_ref[...] = jnp.zeros(token_ref.shape, jnp.float32)


def arrived(pieces):
    return pl.pallas_call(
        arrived_kernel,
        name="arrived",
        in_specs=[pl.BlockSpec(memory_space=pl.ANY)] * 2,
        out_shape=jax.ShapeDtypeStruct((8, 128), jnp.float32),
        compiler_params=pltpu.CompilerParams(vmem_limit_bytes=1024 * 1024),
        cost_estimate=pl.CostEstimate(flops=JOIN_COST, bytes_accessed=4096, transcendentals=0),
    )(*pieces)


def tile_kernel(counts, n_right, places, groups, rows, own_first, n_before, done, n_token, keep, *refs):
    parts, copies = [], []
    n_operands = sum(max(count, 1) for count in counts)
    tail = refs[n_operands + n_before + n_token :]
    outs, kept, tail = tail[:n_right], tail[n_right : n_right + len(keep)], tail[n_right + len(keep) :]
    down, scratch = tail[0], tail[1:]
    keeping = {}

    def put_away(k):
        if k in keep:
            at = keep.index(k)
            keeping[k] = pltpu.make_async_copy(parts[k], kept[at], scratch[-1].at[sum(counts) + at])
            keeping[k].start()

    operands, before = list(refs[:n_operands]), refs[n_operands : n_operands + n_before]
    sem = 0
    for count in counts:
        here, operands = operands[: max(count, 1)], operands[max(count, 1) :]
        if not count:
            parts.append(here[0])
            copies.append([])
            put_away(len(parts) - 1)
            continue
        part, top, own = scratch[sum(1 for c in copies if c)], 0, []
        for piece in here:
            own.append(pltpu.make_async_copy(piece, part.at[pl.ds(top, piece.shape[0])], scratch[-1].at[sem]))
            own[-1].start()
            top, sem = top + piece.shape[0], sem + 1
        parts.append(part)
        copies.append(own)
    for r, out in enumerate(outs):
        out[...] = jnp.full(out.shape, -1.0, jnp.float32)
        if r < n_before:
            out[: before[r].shape[0]] = before[r][...]
    blocks = rows // BLOCK
    labels = {}

    def labels_of(k):
        if k not in labels:
            for copy in copies[k]:
                copy.wait()
            if copies[k]:
                put_away(k)
            label = parts[k][rows:, :rows].astype(jnp.float32)[:1]
            labels[k] = label, label[0, 0], label[0, rows - 1]
        return labels[k]

    def tile(r, c):
        sims = lax.dot_general(
            parts[n_right + c][:rows],
            parts[r][:rows],
            (((1,), (1,)), ((), ())),
            preferred_element_type=jnp.float32,
        )
        for b in range(blocks):
            at = slice(b * BLOCK, (b + 1) * BLOCK)
            label = jnp.concatenate([down[c, at]] * blocks, axis=1)
            same = label == labels[r][0]
            part = sims[at]
            if own_first and c == 0 and r == 0:
                index = lax.broadcasted_iota(jnp.int32, part.shape, 0) + b * BLOCK
                same &= index != lax.broadcasted_iota(jnp.int32, part.shape, 1)
            part = jnp.where(same, part, -1.0)
            row = places[c] + b
            outs[r][row : row + 1, :] = jnp.max(part, axis=0, keepdims=True)

    for group in groups:
        todo = [(r, c) for c in group for r in range(n_right) if r >= n_before or c not in done]
        meet = False
        for r, c in todo:
            right, left = labels_of(r), labels_of(n_right + c)
            meet |= (left[1] <= right[2]) & (right[1] <= left[2])

        def group_tiles(todo=todo):
            for c in sorted({c for _, c in todo}):
                for b in range(blocks):
                    at = slice(b * BLOCK, (b + 1) * BLOCK)
                    down[c, at] = jnp.broadcast_to(labels[n_right + c][0][:, at], (BLOCK, BLOCK)).T
            for r, c in todo:
                tile(r, c)

        if own_first and 0 in group:
            group_tiles()
        else:
            pl.when(meet)(group_tiles)
    for copy in keeping.values():
        copy.wait()


def tiles(name, rights, lefts, places, groups, own_first, before=(), done=(), token=None, flops=None, keep=()):
    parts = list(rights) + list(lefts)
    counts = tuple(len(part) if isinstance(part, list) else 0 for part in parts)
    operands = [piece for part in parts for piece in (part if isinstance(part, list) else [part])]
    height_in, depth = operands[0].shape
    rows = height_in - LABEL_ROWS
    height = -(-(places[-1] + rows // BLOCK) // 8) * 8
    if flops is None:
        flops = 2 * len(rights) * len(lefts) * rows * rows * depth
    vmem, anywhere = pl.BlockSpec(memory_space=pltpu.VMEM), pl.BlockSpec(memory_space=pl.ANY)
    specs = [spec for count in counts for spec in ([anywhere] * count if count else [vmem])]
    extra = list(before) + ([] if token is None else [token])
    scratch = [pltpu.VMEM((len(lefts), rows, BLOCK), jnp.float32)]
    scratch += [pltpu.VMEM((height_in, depth), jnp.bfloat16) for count in counts if count]
    if sum(counts) + len(keep):
        scratch.append(pltpu.SemaphoreType.DMA((sum(counts) + len(keep),)))
    return pl.pallas_call(
        functools.partial(tile_kernel, counts, len(rights), tuple(places), groups, rows, own_first, len(before), done, len(extra) - len(before), keep),
        name=name,
        in_specs=specs + [vmem] * len(extra),
        out_specs=[vmem] * len(rights) + [pl.BlockSpec(memory_space=pltpu.HBM)] * len(keep),
        out_shape=[jax.ShapeDtypeStruct((height, rows), jnp.float32)] * len(rights)
        + [jax.ShapeDtypeStruct((height_in, depth), jnp.bfloat16)] * len(keep),
        scratch_shapes=scratch,
        compiler_params=pltpu.CompilerParams(vmem_limit_bytes=VMEM_TILES),
        cost_estimate=pl.CostEstimate(
            flops=flops, bytes_accessed=2 * len(operands) * rows * depth, transcendentals=0
        ),
    )(*operands, *extra)


def local(embeddings, cluster_id, requests, pair_left, pair_right):
    n = lax.axis_size(AXIS)
    rows = embeddings.shape[0]
    blk_dev = rows // BLOCK

    def swap(x, bit):
        return lax.ppermute(x, AXIS, [(i, i ^ bit) for i in range(n)])

    def from_above(x):
        return lax.ppermute(x, AXIS, [(i + PLANE, i) for i in range(n - PLANE)])

    def from_below(x):
        return lax.ppermute(x, AXIS, [(i, i + PLANE) for i in range(n - PLANE)])

    def owners_best(parts, cap):
        mine, for_x, for_y, for_across = parts
        returned = jnp.stack([mine, swap(for_x, 2), swap(for_y, 4), swap(for_across, 6)])
        return jnp.maximum(jnp.max(jnp.minimum(returned, cap), axis=(0, 1)), -1.0)

    unit = normalise(embeddings, cluster_id)
    along_x, along_y = swap(unit, 2), swap(unit, 4)
    above, below = from_above(unit), from_below(unit)
    twin = swap(unit, 1)
    message = message_of(requests, pair_left, pair_right, cluster_id)
    along_y, _ = lax.optimization_barrier((along_y, message))
    first, second = half_of(along_x, False), half_of(along_y, True)
    pieces = [swap(first, 4), swap(second, 2)]
    along_x, first = lax.optimization_barrier((along_x, first))
    above_twin, below_twin = swap(above, 1), swap(below, 1)

    heard = lax.all_to_all(message, AXIS, split_axis=0, concat_axis=0, tiled=True)

    places = [0, blk_dev] + [8 + blk_dev * k for k in range(4)]
    near_rights = [unit, along_x, along_y]
    known = tiles(
        "plane_tiles",
        near_rights,
        [unit, twin, [above], [below]],
        [places[k] for k in (0, 1, 2, 4)],
        ((0, 1), (2,), (3,)),
        True,
    )
    token = arrived(pieces)
    *parts, across = tiles(
        "all_tiles",
        near_rights + [pieces],
        [unit, twin, [above], above_twin, [below], below_twin],
        places,
        ((0, 1), (2, 3), (4, 5)),
        False,
        known,
        (0, 1, 2, 4),
        token,
        flops=0,
        keep=(3,),
    )
    cap, span = cover(heard, 1, blk_dev, rows)
    best = owners_best(parts, cap)

    def further(best):
        def body(carry):
            offset, best, above, below = carry
            above, below = from_above(above), from_below(below)
            lefts = [above, swap(above, 1), below, swap(below, 1)]
            parts = tiles(
                "further_tiles",
                near_rights + [across],
                lefts,
                [blk_dev * k for k in range(4)],
                ((0, 1), (2, 3)),
                False,
            )
            cap, _ = cover(heard, offset, blk_dev, rows)
            best = jnp.maximum(best, owners_best(parts, cap[:, 8:]))
            return offset + 1, best, above, below

        return lax.while_loop(lambda carry: carry[0] <= span, body, (jnp.int32(2), best, above, below))[1]

    return lax.cond(span >= 2, further, lambda best: best, best)


def solution(mesh):
    in_specs = (P(AXIS, None), P(AXIS), P(AXIS), P(AXIS), P(AXIS))
    return jax.shard_map(local, mesh=mesh, in_specs=in_specs, out_specs=P(AXIS), check_vma=False)
```

```python
import functools

import jax
import jax.numpy as jnp
from jax import lax
from jax.experimental import pallas as pl
from jax.experimental.pallas import tpu as pltpu
from jax.sharding import PartitionSpec as P

BLOCK = 128
CLUSTERS = 16
PLANE = 8
JOIN_COST = 10_000_000_000
AXIS = "dev"
LABEL_ROWS = 16
VMEM_TILES = 8 * 1024 * 1024


def normalise_kernel(x_hbm, cluster_hbm, unit_ref, x_ref, cluster_ref, sems):
    copies = [
        pltpu.make_async_copy(x_hbm, x_ref, sems.at[0]),
        pltpu.make_async_copy(cluster_hbm, cluster_ref, sems.at[1]),
    ]
    for copy in copies:
        copy.start()
    rows, depth = x_ref.shape
    unit_ref[rows:] = jnp.zeros((LABEL_ROWS, depth), jnp.bfloat16)
    copies[1].wait()
    label = (cluster_ref[...] + 1).astype(jnp.bfloat16)
    unit_ref[rows:, :rows] = jnp.broadcast_to(label, (LABEL_ROWS, rows))
    copies[0].wait()
    values = x_ref[...].astype(jnp.float32)
    norm = lax.rsqrt(jnp.sum(values * values, axis=-1, keepdims=True) + 1e-06)
    unit_ref[:rows] = (values * norm).astype(jnp.bfloat16)


def normalise(x, cluster_id):
    rows, depth = x.shape
    return pl.pallas_call(
        normalise_kernel,
        name="normalise",
        in_specs=[pl.BlockSpec(memory_space=pltpu.HBM)] * 2,
        out_shape=jax.ShapeDtypeStruct((rows + LABEL_ROWS, depth), jnp.bfloat16),
        scratch_shapes=[
            pltpu.VMEM((rows, depth), x.dtype),
            pltpu.VMEM((1, rows), jnp.int32),
            pltpu.SemaphoreType.DMA((2,)),
        ],
        compiler_params=pltpu.CompilerParams(vmem_limit_bytes=60 * 1024 * 1024),
    )(x, cluster_id.reshape(1, rows))


def message_kernel(n, left_ref, right_ref, request_ref, cluster_ref, out_ref):
    def dot(a, b):
        return lax.dot_general(a, b, (((1,), (1,)), ((), ())), preferred_element_type=jnp.float32)

    def hot(count, ref):
        index = lax.broadcasted_iota(jnp.int32, (count, ref.shape[1]), 0)
        return (index == ref[...]).astype(jnp.float32).astype(jnp.bfloat16)

    left, right, cluster = hot(n, left_ref), hot(n, right_ref), hot(CLUSTERS, cluster_ref)
    out_ref[...] = jnp.zeros(out_ref.shape, jnp.float32)
    out_ref[:, 0, :n] = dot(left, right) + dot(right, left)
    out_ref[:, 0, n : 2 * n] = jnp.broadcast_to(request_ref[...].astype(jnp.float32), (n, n))
    counts = dot(jnp.ones((n, cluster.shape[1]), jnp.bfloat16), cluster)
    out_ref[:, 0, 2 * n : 2 * n + CLUSTERS] = counts


def message_of(requests, pair_left, pair_right, cluster_id):
    n = requests.shape[0]
    width = -(-(2 * n + CLUSTERS) // BLOCK) * BLOCK
    return pl.pallas_call(
        functools.partial(message_kernel, n),
        name="message",
        out_shape=jax.ShapeDtypeStruct((n, 1, width), jnp.float32),
        compiler_params=pltpu.CompilerParams(vmem_limit_bytes=4 * 1024 * 1024),
    )(pair_left.reshape(1, -1), pair_right.reshape(1, -1), requests.reshape(1, -1), cluster_id.reshape(1, -1))


def cover_kernel(blk_dev, rows, offset_ref, heard_ref, cap_ref, span_ref):
    n = heard_ref.shape[0]
    me = lax.axis_index(AXIS)

    def iota(shape, dimension):
        return lax.broadcasted_iota(jnp.int32, shape, dimension)

    def hot(mask):
        return mask.astype(jnp.float32)

    listed = heard_ref[:, 0, :n] > 0
    requests = heard_ref[:, 0, n : 2 * n]
    own = jnp.sum(jnp.where(iota((n, n), 1) == me, requests, 0.0), axis=1, keepdims=True)
    owns = hot(own == (iota((n, rows), 1) // BLOCK).astype(jnp.float32)).astype(jnp.bfloat16)
    height = cap_ref.shape[1]
    at = iota((4 * height, n), 0)
    source, at = at // height, at % height
    near = at < 8
    at = jnp.where(near, at, at - 8)
    part, block = at // blk_dev, at % blk_dev
    step = jnp.where(near, 0, jnp.where(part < 2, offset_ref[0], -offset_ref[0]))
    device = ((2 * source + part % 2) ^ me) + step * PLANE
    device = jnp.where(near & (part >= 2), -1, device)
    total = jnp.zeros((4 * height, rows), jnp.float32)
    for b in range(blk_dev):
        asked = hot(listed & (requests == b)).T.astype(jnp.bfloat16)
        count = jnp.dot(asked, owns, preferred_element_type=jnp.float32)
        pick = hot((iota((4 * height, n), 1) == device) & (block == b)).astype(jnp.bfloat16)
        total += jnp.dot(pick, hot(count > 0).astype(jnp.bfloat16), preferred_element_type=jnp.float32)
    cap_ref[...] = jnp.where(total > 0, jnp.inf, -1.0).reshape(cap_ref.shape)
    present = heard_ref[:, 0, 2 * n : 2 * n + CLUSTERS] > 0
    plane = (iota((n, CLUSTERS), 0) // PLANE).astype(jnp.float32)
    first = jnp.min(jnp.where(present, plane, float(n)), axis=0, keepdims=True)
    last = jnp.max(jnp.where(present, plane, -1.0), axis=0, keepdims=True)
    span_ref[0] = jnp.max(last - first).astype(jnp.int32)


def cover(heard, offset, blk_dev, rows):
    cap, span = pl.pallas_call(
        functools.partial(cover_kernel, blk_dev, rows),
        name="cover",
        in_specs=[pl.BlockSpec(memory_space=pltpu.SMEM), pl.BlockSpec(memory_space=pltpu.VMEM)],
        out_specs=[pl.BlockSpec(memory_space=pltpu.VMEM), pl.BlockSpec(memory_space=pltpu.SMEM)],
        out_shape=[
            jax.ShapeDtypeStruct((4, 8 + 4 * blk_dev, rows), jnp.float32),
            jax.ShapeDtypeStruct((1,), jnp.int32),
        ],
        compiler_params=pltpu.CompilerParams(vmem_limit_bytes=8 * 1024 * 1024),
    )(jnp.asarray(offset, jnp.int32).reshape(1), heard)
    return cap, span[0]


def half_kernel(top, x_ref, half_ref):
    half_ref[...] = x_ref[top : top + half_ref.shape[0]]


def half_of(x, lower):
    half = (x.shape[0] - LABEL_ROWS) // 2
    return pl.pallas_call(
        functools.partial(half_kernel, half if lower else 0),
        name="lower_half" if lower else "upper_half",
        out_shape=jax.ShapeDtypeStruct((half + LABEL_ROWS * lower, x.shape[1]), x.dtype),
        compiler_params=pltpu.CompilerParams(vmem_limit_bytes=4 * 1024 * 1024),
        cost_estimate=pl.CostEstimate(flops=0, bytes_accessed=x.size * 2, transcendentals=0),
    )(x)


def arrived_kernel(first_ref, second_ref, token_ref):
    del first_ref, second_ref
    token_ref[...] = jnp.zeros(token_ref.shape, jnp.float32)


def arrived(pieces):
    return pl.pallas_call(
        arrived_kernel,
        name="arrived",
        in_specs=[pl.BlockSpec(memory_space=pl.ANY)] * 2,
        out_shape=jax.ShapeDtypeStruct((8, 128), jnp.float32),
        compiler_params=pltpu.CompilerParams(vmem_limit_bytes=1024 * 1024),
        cost_estimate=pl.CostEstimate(flops=JOIN_COST, bytes_accessed=4096, transcendentals=0),
    )(*pieces)


def tile_kernel(counts, n_right, places, groups, rows, own_first, n_before, done, n_token, keep, *refs):
    parts, copies = [], []
    n_operands = sum(max(count, 1) for count in counts)
    tail = refs[n_operands + n_before + n_token :]
    outs, kept, tail = tail[:n_right], tail[n_right : n_right + len(keep)], tail[n_right + len(keep) :]
    down, scratch = tail[0], tail[1:]
    keeping = {}

    def put_away(k):
        if k in keep:
            at = keep.index(k)
            keeping[k] = pltpu.make_async_copy(parts[k], kept[at], scratch[-1].at[sum(counts) + at])
            keeping[k].start()

    operands, before = list(refs[:n_operands]), refs[n_operands : n_operands + n_before]
    sem = 0
    for count in counts:
        here, operands = operands[: max(count, 1)], operands[max(count, 1) :]
        if not count:
            parts.append(here[0])
            copies.append([])
            put_away(len(parts) - 1)
            continue
        part, top, own = scratch[sum(1 for c in copies if c)], 0, []
        for piece in here:
            own.append(pltpu.make_async_copy(piece, part.at[pl.ds(top, piece.shape[0])], scratch[-1].at[sem]))
            own[-1].start()
            top, sem = top + piece.shape[0], sem + 1
        parts.append(part)
        copies.append(own)
    for r, out in enumerate(outs):
        out[...] = jnp.full(out.shape, -1.0, jnp.float32)
        if r < n_before:
            out[: before[r].shape[0]] = before[r][...]
    blocks = rows // BLOCK
    labels = {}

    def labels_of(k):
        if k not in labels:
            for copy in copies[k]:
                copy.wait()
            if copies[k]:
                put_away(k)
            label = parts[k][rows:, :rows].astype(jnp.float32)[:1]
            labels[k] = label, label[0, 0], label[0, rows - 1]
        return labels[k]

    def tile(r, c):
        sims = lax.dot_general(
            parts[n_right + c][:rows],
            parts[r][:rows],
            (((1,), (1,)), ((), ())),
            preferred_element_type=jnp.float32,
        )
        for b in range(blocks):
            at = slice(b * BLOCK, (b + 1) * BLOCK)
            label = jnp.concatenate([down[c, at]] * blocks, axis=1)
            same = label == labels[r][0]
            part = sims[at]
            if own_first and c == 0 and r == 0:
                index = lax.broadcasted_iota(jnp.int32, part.shape, 0) + b * BLOCK
                same &= index != lax.broadcasted_iota(jnp.int32, part.shape, 1)
            part = jnp.where(same, part, -1.0)
            row = places[c] + b
            outs[r][row : row + 1, :] = jnp.max(part, axis=0, keepdims=True)

    for group in groups:
        todo = [(r, c) for c in group for r in range(n_right) if r >= n_before or c not in done]
        meet = False
        for r, c in todo:
            right, left = labels_of(r), labels_of(n_right + c)
            meet |= (left[1] <= right[2]) & (right[1] <= left[2])

        def group_tiles(todo=todo):
            for c in sorted({c for _, c in todo}):
                for b in range(blocks):
                    at = slice(b * BLOCK, (b + 1) * BLOCK)
                    down[c, at] = jnp.broadcast_to(labels[n_right + c][0][:, at], (BLOCK, BLOCK)).T
            for r, c in todo:
                tile(r, c)

        if own_first and 0 in group:
            group_tiles()
        else:
            pl.when(meet)(group_tiles)
    for copy in keeping.values():
        copy.wait()


def tiles(name, rights, lefts, places, groups, own_first, before=(), done=(), token=None, flops=None, keep=()):
    parts = list(rights) + list(lefts)
    counts = tuple(len(part) if isinstance(part, list) else 0 for part in parts)
    operands = [piece for part in parts for piece in (part if isinstance(part, list) else [part])]
    height_in, depth = operands[0].shape
    rows = height_in - LABEL_ROWS
    height = -(-(places[-1] + rows // BLOCK) // 8) * 8
    if flops is None:
        flops = 2 * len(rights) * len(lefts) * rows * rows * depth
    vmem, anywhere = pl.BlockSpec(memory_space=pltpu.VMEM), pl.BlockSpec(memory_space=pl.ANY)
    specs = [spec for count in counts for spec in ([anywhere] * count if count else [vmem])]
    extra = list(before) + ([] if token is None else [token])
    scratch = [pltpu.VMEM((len(lefts), rows, BLOCK), jnp.float32)]
    scratch += [pltpu.VMEM((height_in, depth), jnp.bfloat16) for count in counts if count]
    if sum(counts) + len(keep):
        scratch.append(pltpu.SemaphoreType.DMA((sum(counts) + len(keep),)))
    return pl.pallas_call(
        functools.partial(tile_kernel, counts, len(rights), tuple(places), groups, rows, own_first, len(before), done, len(extra) - len(before), keep),
        name=name,
        in_specs=specs + [vmem] * len(extra),
        out_specs=[vmem] * len(rights) + [pl.BlockSpec(memory_space=pltpu.HBM)] * len(keep),
        out_shape=[jax.ShapeDtypeStruct((height, rows), jnp.float32)] * len(rights)
        + [jax.ShapeDtypeStruct((height_in, depth), jnp.bfloat16)] * len(keep),
        scratch_shapes=scratch,
        compiler_params=pltpu.CompilerParams(vmem_limit_bytes=VMEM_TILES),
        cost_estimate=pl.CostEstimate(
            flops=flops, bytes_accessed=2 * len(operands) * rows * depth, transcendentals=0
        ),
    )(*operands, *extra)


def local(embeddings, cluster_id, requests, pair_left, pair_right):
    n = lax.axis_size(AXIS)
    rows = embeddings.shape[0]
    blk_dev = rows // BLOCK

    def swap(x, bit):
        return lax.ppermute(x, AXIS, [(i, i ^ bit) for i in range(n)])

    def from_above(x):
        return lax.ppermute(x, AXIS, [(i + PLANE, i) for i in range(n - PLANE)])

    def from_below(x):
        return lax.ppermute(x, AXIS, [(i, i + PLANE) for i in range(n - PLANE)])

    def owners_best(parts, cap):
        mine, for_x, for_y, for_across = parts
        best = jnp.maximum(jnp.max(jnp.minimum(mine, cap[0]), axis=0), -1.0)
        for k, (part, bit) in enumerate(((for_across, 6), (for_y, 4), (for_x, 2))):
            best = jnp.maximum(best, jnp.max(jnp.minimum(swap(part, bit), cap[3 - k]), axis=0))
        return best

    unit = normalise(embeddings, cluster_id)
    along_x, along_y = swap(unit, 2), swap(unit, 4)
    above, below = from_above(unit), from_below(unit)
    twin = swap(unit, 1)
    message = message_of(requests, pair_left, pair_right, cluster_id)
    along_y, _ = lax.optimization_barrier((along_y, message))
    first, second = half_of(along_x, False), half_of(along_y, True)
    pieces = [swap(first, 4), swap(second, 2)]
    along_x, first = lax.optimization_barrier((along_x, first))
    above_twin, below_twin = swap(above, 1), swap(below, 1)

    heard = lax.all_to_all(message, AXIS, split_axis=0, concat_axis=0, tiled=True)

    places = [0, blk_dev] + [8 + blk_dev * k for k in range(4)]
    near_rights = [unit, along_x, along_y]
    known = tiles(
        "plane_tiles",
        near_rights,
        [unit, twin, [above], [below]],
        [places[k] for k in (0, 1, 2, 4)],
        ((0, 1), (2,), (3,)),
        True,
    )
    token = arrived(pieces)
    *parts, across = tiles(
        "all_tiles",
        near_rights + [pieces],
        [unit, twin, [above], above_twin, [below], below_twin],
        places,
        ((0, 1), (2, 3), (4, 5)),
        False,
        known,
        (0, 1, 2, 4),
        token,
        flops=0,
        keep=(3,),
    )
    cap, span = cover(heard, 1, blk_dev, rows)
    best = owners_best(parts, cap)

    def further(best):
        def body(carry):
            offset, best, above, below = carry
            above, below = from_above(above), from_below(below)
            lefts = [above, swap(above, 1), below, swap(below, 1)]
            parts = tiles(
                "further_tiles",
                near_rights + [across],
                lefts,
                [blk_dev * k for k in range(4)],
                ((0, 1), (2, 3)),
                False,
            )
            cap, _ = cover(heard, offset, blk_dev, rows)
            best = jnp.maximum(best, owners_best(parts, cap[:, 8:]))
            return offset + 1, best, above, below

        return lax.while_loop(lambda carry: carry[0] <= span, body, (jnp.int32(2), best, above, below))[1]

    return lax.cond(span >= 2, further, lambda best: best, best)


def solution(mesh):
    in_specs = (P(AXIS, None), P(AXIS), P(AXIS), P(AXIS), P(AXIS))
    return jax.shard_map(local, mesh=mesh, in_specs=in_specs, out_specs=P(AXIS), check_vma=False)
```
